512 devices in a mesh: dom: 16 (over z_hi, y, core), edge: 32 (over z_lo, x).
Axes of the slice: x: 4, y: 4, z: 16 (z_hi: 2, z_lo: 8; z = z_hi * 8 + z_lo), core: 2. Of those that a mesh axis runs over, the one named last changes fastest.
Arguments:
- entities: float32 [65536, 400], P(('dom', 'edge')), may hold values from -2 to 2
- entity_state: float32 [65536], P(('dom', 'edge')), may hold values from 0.0001 to 0.1
- relations: float32 [672, 400], replicated, may hold values from -4 to 4
- relation_state: float32 [672, 400], replicated, may hold values from 0.01 to 1
- live_blocks: int32 [2, 512], P(None, ('dom', 'edge')), may hold values from 1 to 10, as said below
- dst_blocks: int32 [2, 5120], P(None, ('dom', 'edge')), may hold values from 0 to 31
- relation_ids: int32 [2, 5120], P(None, ('dom', 'edge')), may hold values from 0 to 671
- source_rows: int32 [2, 5120, 128], P(None, ('dom', 'edge')), may hold values from 0 to 127
- target_rows: int32 [2, 5120, 128], P(None, ('dom', 'edge')), may hold values from 0 to 127
- negative_blocks: int32 [2, 5120, 4], P(None, ('dom', 'edge')), may hold values from 0 to 31
Outputs:
- new_entities: float32 [65536, 400], P(('dom', 'edge'))
- new_entity_state: float32 [65536], P(('dom', 'edge'))
- new_relations: float32 [672, 400], replicated
- new_relation_state: float32 [672, 400], replicated
The draws below stay inside these ranges and needn't reach their ends.
Inputs may be any that keep to these rules, and one draw needn't show every extreme that they name: live_blocks[r, v] slots of device v are used in round r; in every round some device uses all 10 of them.
All inputs are finite; a program needn't handle non-finite values.
Results may differ from the reference program's by a relative error of at most 0.008.
Values may be sent and summed in bfloat16 or wider, within the bound.
No kernel may reach another device: no remote copies, remote signals or barrier semaphores. Data moves between devices by JAX's collectives and lax.ppermute only.
A program may use at most 128 MiB of HBM per device.

```python
import math
import jax
import jax.numpy as jnp
import numpy as np
from jax import lax

DIM = 400
REL = 672
BLOCK = 128
NEG = 4
ROUNDS = 2
NB = 10
PART_BLOCKS = 32
ENTITIES = 65536
EDGE_BLOCKS = 5120
N_DOM = 16
N_EDGE = 32
DEVICES = 512


def draw_live_blocks(key, part):
    key = jax.random.fold_in(key, 11)
    first, second, third = jax.random.split(key, 3)
    left = jax.random.randint(first, (ROUNDS, DEVICES), 0, NB)
    right = jax.random.randint(second, (ROUNDS, DEVICES), 0, NB)
    counts = 1 + left * right // NB
    fullest = jax.random.randint(third, (ROUNDS,), 0, DEVICES)
    places = jnp.arange(DEVICES, dtype=jnp.int32)
    return jnp.where(places[None, :] == fullest[:, None], NB, counts).astype(jnp.int32)


def set_ends(array, rng, least, largest):
    place = [jax.random.randint(jax.random.fold_in(rng, axis), (), 0, length) for axis, length in enumerate(array.shape)]
    longest = array.shape.index(max(array.shape))
    next_to = place[:longest] + [(place[longest] + 1) % array.shape[longest]] + place[longest + 1:]
    return array.at[tuple(place)].set(least).at[tuple(next_to)].set(largest)


def level_of(stream_key, dims, cuts, low, largest):
    gain, own = 1.0, jax.random.fold_in(stream_key, 6)
    for position, parts in cuts:
        draws = jnp.exp(jax.random.uniform(jax.random.fold_in(own, position), (parts,), jnp.float32, low / len(cuts), largest / len(cuts)))
        gain = gain * jnp.repeat(draws, dims[position] // parts).reshape([-1 if axis == position else 1 for axis in range(len(dims))])
    return gain


def rank_table(number_of, slope):
    weights = [(1 << 20) // math.isqrt(grade ** slope) + 1 for grade in range(1, number_of + 1)]
    deviation = 1 + sum(weights) // (1 << 30)
    return np.cumsum(np.array([max(1, weight // deviation) for weight in weights]))


def ranked(own_key, dims, number_of, skew):
    listing = rank_table(number_of, skew)
    pick = jax.random.randint(jax.random.fold_in(own_key, 1), dims, 0, int(listing[number_of - 1]))
    rank = jnp.searchsorted(jnp.asarray(listing, jnp.int32), pick, side="right")
    return jax.random.permutation(jax.random.fold_in(own_key, 2), number_of)[rank].astype(jnp.int32)


def bell_draw(key, shape, spread, reach, pieces=(), kind=jnp.bfloat16):
    drawn = jax.random.normal(key, shape, jnp.float32) * spread
    if len(pieces) > 0:
        drawn = level_of(key, shape, pieces, -0.22, 0.18) * drawn
    return jnp.clip(drawn, min=-reach, max=reach).astype(kind)


def setup_inputs(seed: int = 0) -> dict:
    arg_keys = jax.random.split(jax.random.key(seed), 11)
    return {
        "entities": bell_draw(arg_keys[0], (ENTITIES, DIM), 0.3, 2.0, ((0, 512),), jnp.float32),
        "entity_state": jnp.clip(jnp.exp(math.log(0.1) - 6.9077553 * jax.random.uniform(arg_keys[1], (ENTITIES,), jnp.float32) ** level_of(arg_keys[1], (ENTITIES,), ((0, 512),), -0.2, 0.2)), 0.0001, 0.1),
        "relations": bell_draw(arg_keys[2], (REL, DIM), 0.7, 4.0, (), jnp.float32),
        "relation_state": jnp.clip(jnp.exp(jax.random.uniform(arg_keys[3], (REL, DIM), jnp.float32, math.log(0.01), math.log(1.0))), 0.01, 1.0),
        "live_blocks": draw_live_blocks(jax.random.fold_in(arg_keys[10], 71), 0),
        "dst_blocks": set_ends(jax.random.randint(arg_keys[5], (ROUNDS, EDGE_BLOCKS), 0, PART_BLOCKS), jax.random.fold_in(arg_keys[5], 1), 0, PART_BLOCKS - 1).astype(jnp.int32),
        "relation_ids": set_ends(ranked(arg_keys[6], (ROUNDS, EDGE_BLOCKS), REL, 2), jax.random.fold_in(arg_keys[6], 3), 0, REL - 1).astype(jnp.int32),
        "source_rows": set_ends(jax.random.randint(arg_keys[7], (ROUNDS, EDGE_BLOCKS, BLOCK), 0, BLOCK), jax.random.fold_in(arg_keys[7], 1), 0, BLOCK - 1).astype(jnp.int32),
        "target_rows": set_ends(jax.random.randint(arg_keys[8], (ROUNDS, EDGE_BLOCKS, BLOCK), 0, BLOCK), jax.random.fold_in(arg_keys[8], 1), 0, BLOCK - 1).astype(jnp.int32),
        "negative_blocks": set_ends(jax.random.randint(arg_keys[9], (ROUNDS, EDGE_BLOCKS, NEG), 0, PART_BLOCKS), jax.random.fold_in(arg_keys[9], 1), 0, PART_BLOCKS - 1).astype(jnp.int32),
    }


ENT_RATE = 0.25
REL_RATE = 0.25

def edge_block(own_rows, part3, relations, rel, src, tgt, dst, negs):
    block, width = own_rows.shape
    half = width // 2
    places = jnp.arange(block, dtype=jnp.int32)
    src_hot = (src[:, None] == places[None, :]).astype(jnp.bfloat16)
    tgt_hot = (tgt[:, None] == places[None, :]).astype(jnp.bfloat16)
    heads = jnp.dot(src_hot, own_rows, preferred_element_type=jnp.float32)
    target_block = lax.dynamic_index_in_dim(part3, dst, 0, keepdims=False)
    tails = jnp.dot(tgt_hot, target_block, preferred_element_type=jnp.float32)
    operator = lax.dynamic_index_in_dim(relations, rel, 0, keepdims=False)
    h_re, h_im = (heads[:, :half], heads[:, half:])
    r_re, r_im = (operator[:half], operator[half:])
    query = jnp.concatenate([h_re * r_re - h_im * r_im, h_re * r_im + h_im * r_re], 1).astype(jnp.bfloat16)
    query_f = query.astype(jnp.float32)
    positive = lax.optimization_barrier(jnp.sum(query_f * tails, 1))
    negatives = jnp.take(part3, negs, axis=0).reshape(-1, width)
    scores = lax.dot_general(query, negatives, (((1,), (1,)), ((), ())), preferred_element_type=jnp.float32)
    pos_weight = -jax.nn.sigmoid(-positive)
    neg_weight = (jax.nn.sigmoid(scores) / scores.shape[1]).astype(jnp.bfloat16)
    grad_query = pos_weight[:, None] * tails + jnp.dot(neg_weight, negatives, preferred_element_type=jnp.float32)
    tgt_add = jnp.zeros((block, width), jnp.float32).at[tgt].add(pos_weight[:, None] * query_f)
    neg_add = lax.dot_general(neg_weight, query, (((0,), (0,)), ((), ())), preferred_element_type=jnp.float32)
    neg_add = neg_add.reshape(negs.shape[0], block, width)
    g_re, g_im = (grad_query[:, :half], grad_query[:, half:])
    head_grad = jnp.concatenate([g_re * r_re + g_im * r_im, g_im * r_re - g_re * r_im], 1)
    lhs_add = jnp.zeros((block, width), jnp.float32).at[src].add(head_grad)
    rel_add = jnp.concatenate([lax.optimization_barrier(jnp.sum(g_re * h_re + g_im * h_im, 0)), lax.optimization_barrier(jnp.sum(g_im * h_re - g_re * h_im, 0))])
    return (lhs_add, tgt_add, neg_add, rel_add)

def reference(entities, entity_state, relations, relation_state, live_blocks, dst_blocks, relation_ids, source_rows, target_rows, negative_blocks):
    weights, state, rel, rel_state = (entities, entity_state, relations, relation_state)
    width = weights.shape[1]
    part_rows = N_EDGE * BLOCK
    for r in range(ROUNDS):
        table = weights.astype(jnp.bfloat16)

        def device(carry, dev):
            rhs_total, lhs_total, rel_total = carry
            dom = dev // N_EDGE
            own_rows = lax.dynamic_slice_in_dim(table, (dev * BLOCK).astype(jnp.int32), BLOCK, 0)
            visit = ((dom + r) % N_DOM).astype(jnp.int32)
            part3 = lax.dynamic_slice_in_dim(table, visit * part_rows, part_rows, 0).reshape(N_EDGE, BLOCK, width)
            count = live_blocks[r, dev]

            def step(j, inner):
                rhs_part, lhs_part, rel_sum = inner
                slot = dev * NB + j
                rel_id = relation_ids[r, slot]
                negs = negative_blocks[r, slot]
                dst = dst_blocks[r, slot]
                lhs_add, tgt_add, neg_add, rel_add = edge_block(own_rows, part3, rel, rel_id, source_rows[r, slot], target_rows[r, slot], dst, negs)
                rhs_part = rhs_part.at[dst].add(tgt_add)
                rhs_part = rhs_part.at[negs].add(neg_add)
                return (rhs_part, lhs_part + lhs_add, rel_sum.at[rel_id].add(rel_add))
            init = (jnp.zeros((N_EDGE, BLOCK, width), jnp.float32), jnp.zeros((BLOCK, width), jnp.float32), rel_total)
            rhs_part, lhs_part, rel_total = lax.fori_loop(0, count, step, init)
            rounded = lax.optimization_barrier(rhs_part.reshape(part_rows, width).astype(jnp.bfloat16)).astype(jnp.float32)
            current = lax.dynamic_slice_in_dim(rhs_total, visit * part_rows, part_rows, 0)
            rhs_total = lax.dynamic_update_slice_in_dim(rhs_total, current + rounded, visit * part_rows, 0)
            lhs_total = lax.dynamic_update_slice_in_dim(lhs_total, lhs_part, (dev * BLOCK).astype(jnp.int32), 0)
            return ((rhs_total, lhs_total, rel_total), None)
        init = (jnp.zeros(weights.shape, jnp.float32), jnp.zeros(weights.shape, jnp.float32), jnp.zeros(rel.shape, jnp.float32))
        (rhs_total, lhs_total, rel_total), _ = lax.scan(device, init, jnp.arange(N_DOM * N_EDGE, dtype=jnp.int32))
        grads = lhs_total + rhs_total
        state = state + lax.optimization_barrier(jnp.mean(grads * grads, axis=1))
        weights = weights - ENT_RATE * grads / jnp.sqrt(state)[:, None]
        rel_state = rel_state + rel_total * rel_total
        rel = rel - REL_RATE * rel_total / jnp.sqrt(rel_state)
    return (weights, state, rel, rel_state)
```

```python
import jax
import jax.numpy as jnp
from jax import lax
from jax.experimental import pallas as pl
from jax.experimental.pallas import tpu as pltpu
from jax.sharding import PartitionSpec as P

AXES = ("dom", "edge")
N_DOM, N_EDGE = 16, 32
ENT_RATE = 0.25
REL_RATE = 0.25
F32, BF16 = jnp.float32, jnp.bfloat16
GROUP = 16
PIECE = 80
FOLD = 112
DIGIT = 32
LISTS = 32
MIB = 1024 * 1024


def coords(v):
    dom, edge = v // N_EDGE, v % N_EDGE
    return edge % 4, (dom // 2) % 4, dom // 8, edge // 4, dom % 2


def place(x, y, z_hi, z_lo, core):
    return ((z_hi * 4 + y) * 2 + core) * N_EDGE + z_lo * 4 + x


def turn(v):
    x, y, z_hi, z_lo, core = coords(v)
    return place(x, z_lo % 4, z_hi, y + 4 * core, z_lo // 4)


def ahead(v):
    dom, edge = v // N_EDGE, v % N_EDGE
    return turn((dom + 1) % N_DOM * N_EDGE + edge)


ALL = range(N_DOM * N_EDGE)
TURN = [(v, turn(v)) for v in ALL]
AHEAD = [(v, ahead(v)) for v in ALL]
BACK = [(ahead(v), v) for v in ALL]
NEXT = [(turn(v), ahead(v)) for v in ALL]


OTHER = []
for v in ALL:
    x, y, z_hi, z_lo, core = coords(v)
    OTHER.append((v, place(x, y, z_hi, z_lo, 1 - core)))

PLANES = [[place(c % 4, c // 4 % 4, z // 8, z % 8, c // 16) for c in range(32)] for z in range(16)]
SHEETS = [plane[16 * core : 16 * core + 16] for plane in PLANES for core in range(2)]


def z_pairs(step):
    pairs = []
    for v in ALL:
        x, y, z_hi, z_lo, core = coords(v)
        z = (z_hi * 8 + z_lo) ^ step
        pairs.append((v, place(x, y, z // 8, z % 8, core)))
    return pairs


def send(value, pairs):
    return lax.ppermute(value, AXES, pairs)


def exchange(value, groups):
    return lax.all_to_all(value, AXES, 0, 0, axis_index_groups=groups, tiled=True)


def gather_sheet(own):
    return exchange(jnp.broadcast_to(own, (16,) + own.shape), SHEETS)


def together(*values):
    return lax.optimization_barrier(values)


def nt(a, b):
    return lax.dot_general(a, b, (((1,), (1,)), ((), ())), preferred_element_type=F32)


def nn(a, b):
    return jnp.dot(a, b, preferred_element_type=F32)


def blocks_kernel(
    scal, here, lists, own, rel, half, other, mine_out, theirs_out, lhs_out, rel_out, table, acc, rel_acc, sems
):
    slots = 10
    width, block = own.shape
    mid = width // 2
    copies = [
        pltpu.make_async_copy(src, table.at[pl.ds(16 * i, 16)], sems.at[i])
        for i, src in enumerate((half, other))
    ]
    for copy in copies:
        copy.start()

    def clear(k, carry):
        acc[k] = jnp.zeros((width, block), F32)
        return carry

    lax.fori_loop(0, 32, clear, 0)
    rel_acc[...] = jnp.zeros(rel_acc.shape, F32)
    lhs_out[...] = jnp.zeros(lhs_out.shape, F32)
    for copy in copies:
        copy.wait()

    def near(b):
        return ((b >> 4) ^ here[0]) * 16 + (b & 15)

    rows = lax.broadcasted_iota(jnp.int32, (block, block), 0)
    lanes = lax.broadcasted_iota(jnp.int32, (block, block), 1)

    def step(j, carry):
        src_hot = jnp.where(rows == lists[pl.ds(j, 1), :], 1.0, 0.0).astype(BF16)
        tgt_hot = jnp.where(rows == lists[pl.ds(slots + j, 1), :], 1.0, 0.0).astype(BF16)
        dst, rel_id = near(scal[j]), scal[slots + j] * DIGIT + scal[2 * slots + j]
        negs = [near(scal[3 * slots + 4 * j + i]) for i in range(4)]
        rel_tile = pl.ds(pl.multiple_of((rel_id >> 7) * 128, 128), 128)
        rel_row = jnp.where(rows == (rel_id & 127), 1.0, 0.0).astype(BF16)
        rel_lane = jnp.where(lanes == (rel_id & 127), 1.0, 0.0).astype(BF16)
        heads = nn(own[...], src_hot)
        tails = nn(table[dst], tgt_hot)
        rel_value = rel[:, rel_tile]
        high = rel_value.astype(BF16)
        low = (rel_value - high.astype(F32)).astype(BF16)
        op = nn(high, rel_row) + nn(low, rel_row)
        h_re, h_im = heads[:mid], heads[mid:]
        r_re, r_im = op[:mid], op[mid:]
        query = jnp.concatenate([h_re * r_re - h_im * r_im, h_re * r_im + h_im * r_re], 0).astype(BF16)
        query_f = query.astype(F32)
        positive = jnp.sum(query_f * tails, 0, keepdims=True)
        neg_rows = jnp.concatenate([table[n] for n in negs], 1)
        scores = nn(query_f.T.astype(BF16), neg_rows)
        pos_weight = -jax.nn.sigmoid(-positive)
        neg_weight = (jax.nn.sigmoid(scores) * (1.0 / scores.shape[1])).astype(BF16)
        grad_query = pos_weight * tails + nt(neg_rows, neg_weight)
        neg_add = nn(query, neg_weight)
        for i, n in enumerate(negs):
            acc[n] += neg_add[:, block * i : block * (i + 1)]
        acc[dst] += nt((pos_weight * query_f).astype(BF16), tgt_hot)
        g_re, g_im = grad_query[:mid], grad_query[mid:]
        head_grad = jnp.concatenate([g_re * r_re + g_im * r_im, g_im * r_re - g_re * r_im], 0)
        lhs_out[...] += nt(head_grad.astype(BF16), src_hot)
        op_grad = jnp.concatenate([g_re * h_re + g_im * h_im, g_im * h_re - g_re * h_im], 0)
        rel_acc[:, rel_tile] += nn(op_grad.astype(BF16), rel_lane)
        return carry

    lax.fori_loop(0, scal[7 * slots], step, 0)

    def pack(k, carry):
        mine_out[k] = acc[k].astype(BF16)
        theirs_out[k] = acc[16 + k].astype(BF16)
        return carry

    lax.fori_loop(0, 16, pack, 0)
    tiles = rel_acc.shape[1] // block
    for t in range(tiles - 1):
        rel_out[width * t : width * (t + 1)] = rel_acc[:, block * t : block * (t + 1)].astype(BF16)
    tail = rel_acc[:, block * (tiles - 1) :]
    folded = tail[:FOLD]
    for q in range(1, 4):
        part = tail[FOLD * q : FOLD * (q + 1)]
        if part.shape[0] < FOLD:
            part = jnp.concatenate([part, jnp.zeros((FOLD - part.shape[0], block), F32)], 0)
        folded = folded + pltpu.roll(part, q * block // 4, 1)
    first = width * (tiles - 1)
    rel_out[first : first + FOLD] = folded.astype(BF16)
    rel_out[first + FOLD :] = jnp.zeros((rel_out.shape[0] - first - FOLD, block), BF16)


def run_blocks(lists, here, own, rel, half, other):
    width, block = own.shape
    rel_lanes = rel.shape[1]
    vmem = pl.BlockSpec(memory_space=pltpu.VMEM)
    smem = pl.BlockSpec(memory_space=pltpu.SMEM)
    hbm = pl.BlockSpec(memory_space=pl.ANY)
    return pl.pallas_call(
        blocks_kernel,
        out_shape=(
            jax.ShapeDtypeStruct((16, width, block), BF16),
            jax.ShapeDtypeStruct((16, width, block), BF16),
            jax.ShapeDtypeStruct((width, block), F32),
            jax.ShapeDtypeStruct((32 * PIECE, block), BF16),
        ),
        in_specs=[smem, smem, vmem, vmem, vmem, hbm, hbm],
        out_specs=(vmem, vmem, vmem, vmem),
        scratch_shapes=[
            pltpu.VMEM((32, width, block), BF16),
            pltpu.VMEM((32, width, block), F32),
            pltpu.VMEM((width, rel_lanes), F32),
            pltpu.SemaphoreType.DMA((2,)),
        ],
        compiler_params=pltpu.CompilerParams(vmem_limit_bytes=40 * MIB),
        cost_estimate=pl.CostEstimate(flops=2 * 10**9, bytes_accessed=10**7, transcendentals=10**6),
        name="edge_blocks",
    )(lists[20], here, lists, own, rel, half, other)


def adagrad(grads, kept):
    width = grads.shape[0]
    state = kept[width : width + 1] + jnp.sum(grads * grads, 0, keepdims=True) * (1.0 / width)
    weights = kept[:width] - grads * (ENT_RATE / jnp.sqrt(state))
    return weights, state


def add_pieces(pieces):
    def add(k, total):
        return total + pieces[k].astype(F32)

    return lax.fori_loop(1, pieces.shape[0], add, pieces[0].astype(F32))


def middle_kernel(pieces, lhs, kept, kept_out, table_out):
    width = lhs.shape[0]
    weights, state = adagrad(lhs[...] + add_pieces(pieces), kept[...])
    kept_out[:width] = weights
    kept_out[width:] = jnp.broadcast_to(state, (kept.shape[0] - width, state.shape[1]))
    table_out[...] = weights.astype(BF16)


def middle(pieces, lhs, kept):
    return pl.pallas_call(
        middle_kernel,
        out_shape=(jax.ShapeDtypeStruct(kept.shape, F32), jax.ShapeDtypeStruct(lhs.shape, BF16)),
        compiler_params=pltpu.CompilerParams(vmem_limit_bytes=16 * MIB),
        name="middle_update",
    )(pieces, lhs, kept)


def fold_kernel(pieces, out):
    out[...] = add_pieces(pieces).astype(out.dtype)


def fold(pieces, kind):
    return pl.pallas_call(
        fold_kernel,
        out_shape=jax.ShapeDtypeStruct(pieces.shape[1:], kind),
        compiler_params=pltpu.CompilerParams(vmem_limit_bytes=16 * MIB),
        name="fold_pieces",
    )(pieces)


def last_kernel(rhs, lhs, kept, weights_out, state_out):
    weights, state = adagrad(rhs[...].astype(F32) + lhs[...].astype(F32), kept[...])
    weights_out[...] = weights
    state_out[...] = state


def last(rhs, lhs, kept):
    width, block = lhs.shape
    return pl.pallas_call(
        last_kernel,
        out_shape=(
            jax.ShapeDtypeStruct((width, block), F32),
            jax.ShapeDtypeStruct((1, block), F32),
        ),
        name="last_update",
    )(rhs, lhs, kept)


def z_step(total, step, kind):
    mine = total.astype(kind)
    return mine.astype(F32) + send(mine, z_pairs(step)).astype(F32)


def exchange_terms(mine, theirs, rel_part):
    swapped = send(theirs, OTHER)
    rel_pieces = exchange(rel_part.reshape(32, PIECE, -1), PLANES)
    summed, rel_pieces = together(mine + swapped, rel_pieces)
    rel_mine = fold(rel_pieces, F32)
    for step, kind in ((1, F32), (2, F32), (4, BF16)):
        rel_mine = z_step(rel_mine, step, kind)
    return exchange(summed, SHEETS), rel_mine


def spread_relations(mine):
    mine = mine.astype(BF16)
    return exchange(jnp.broadcast_to(mine, (32,) + mine.shape), PLANES)


def relation_kernel(packed, rel, rel_state, rel_out, state_out):
    width, count = rel_state.shape
    block = packed.shape[1]
    tiles = -(-count // block)
    rest = count - block * (tiles - 1)

    def update(grads, rows, lanes):
        state = rel_state[rows, lanes] + grads * grads
        state_out[rows, lanes] = state
        rel_out[rows, lanes] = rel[rows, lanes] - REL_RATE * grads / jnp.sqrt(state)

    def full(p, carry):
        for t in range(tiles - 1):
            grads = packed[pl.ds(pl.multiple_of(width * t + p * GROUP, GROUP), GROUP), :].astype(F32)
            rows = pl.ds(pl.multiple_of(p * GROUP, GROUP), GROUP)
            update(grads, rows, slice(block * t, block * (t + 1)))
        return carry

    lax.fori_loop(0, width // GROUP, full, 0)
    first = width * (tiles - 1)
    folded = packed[first : first + FOLD, :].astype(F32)
    for q in range(4):
        stop = min(FOLD * (q + 1), width)
        grads = folded if q == 0 else pltpu.roll(folded, block - q * block // 4, 1)
        lanes = slice(block * (tiles - 1), count)
        update(grads[: stop - FOLD * q, :rest], slice(FOLD * q, stop), lanes)
    if rel_out.shape[1] > count:
        rel_out[:, count:] = jnp.zeros((width, rel_out.shape[1] - count), F32)


def relation_update(pieces, rel, rel_state, lanes):
    width = rel.shape[0]
    return pl.pallas_call(
        relation_kernel,
        out_shape=(
            jax.ShapeDtypeStruct((width, lanes), F32),
            jax.ShapeDtypeStruct(rel_state.shape, F32),
        ),
        compiler_params=pltpu.CompilerParams(vmem_limit_bytes=16 * MIB),
        name="relation_update",
    )(pieces.reshape(-1, pieces.shape[2]), rel, rel_state)


def shards(
    entities,
    entity_state,
    relations,
    relation_state,
    live_blocks,
    dst_blocks,
    relation_ids,
    source_rows,
    target_rows,
    negative_blocks,
):
    block, width = entities.shape
    dom = lax.axis_index("dom")
    here = (dom % 2).astype(jnp.int32)[None]

    def lists_of(r):
        ids = relation_ids[r]
        numbers = [dst_blocks[r], ids // DIGIT, ids % DIGIT, negative_blocks[r].reshape(-1), live_blocks[r]]
        numbers = jnp.concatenate(numbers)
        numbers = jnp.pad(numbers, (0, block - numbers.shape[0]))[None]
        rows = jnp.concatenate([source_rows[r], target_rows[r], numbers])
        return jnp.pad(rows, ((0, LISTS - rows.shape[0]), (0, 0))).astype(BF16)

    weights = entities.T
    own = send(weights.astype(BF16), TURN)
    lists = send(jnp.concatenate([lists_of(0), lists_of(1)]), TURN)
    kept = send(jnp.concatenate([weights, jnp.broadcast_to(entity_state[None], (8, block))]), TURN)

    count = relations.shape[0]
    lanes = -(-count // block) * block
    rel = jnp.pad(relations.T, ((0, 0), (0, lanes - count)))
    rel_state = relation_state.T

    half, lists, kept = together(gather_sheet(own), lists, kept)
    other = send(half, OTHER)
    mine, theirs, lhs, rel_part = run_blocks(lists[:LISTS].astype(jnp.int32), here, own, rel, half, other)
    pieces, rel_mine = together(*exchange_terms(mine, theirs, rel_part))
    kept, own = middle(pieces, lhs, kept)
    source = send(jnp.concatenate([own, lists[LISTS:]]), NEXT)
    kept = send(kept, TURN)
    half, source, rel_mine = together(gather_sheet(own), source, z_step(rel_mine, 8, BF16))
    other = send(half, OTHER)
    rel, rel_state = relation_update(spread_relations(rel_mine), rel, rel_state, lanes)
    other, kept = together(other, kept)

    lists = source[width:].astype(jnp.int32)
    mine, theirs, lhs, rel_part = run_blocks(lists, here, source[:width], rel, half, other)
    pieces, rel_mine = exchange_terms(mine, theirs, rel_part)
    rel_sum = spread_relations(z_step(rel_mine, 8, BF16))
    rhs, lhs = together(fold(pieces, BF16), lhs.astype(BF16))
    weights, state = last(send(rhs, TURN), send(lhs, BACK), kept)
    rel, rel_state = relation_update(rel_sum, rel, rel_state, count)
    return (weights.T, state[0], rel.T, rel_state.T)


def solution(mesh):
    placed = (
        P(AXES, None),
        P(AXES),
        P(),
        P(),
        P(None, AXES),
        P(None, AXES),
        P(None, AXES),
        P(None, AXES, None),
        P(None, AXES, None),
        P(None, AXES, None),
    )
    return jax.shard_map(
        shards,
        mesh=mesh,
        in_specs=placed,
        out_specs=(P(AXES, None), P(AXES), P(), P()),
        check_vma=False,
    )
```

```python
import functools

import jax
import jax.numpy as jnp
from jax import lax
from jax.experimental import pallas as pl
from jax.experimental.pallas import tpu as pltpu
from jax.sharding import PartitionSpec as P

AXES = ("dom", "edge")
N_DOM, N_EDGE = 16, 32
ENT_RATE = 0.25
REL_RATE = 0.25
F32, BF16 = jnp.float32, jnp.bfloat16
GROUP = 16
PIECE = 80
FOLD = 112
DIGIT = 32
LISTS = 32
MIB = 1024 * 1024


def coords(v):
    dom, edge = v // N_EDGE, v % N_EDGE
    return edge % 4, (dom // 2) % 4, dom // 8, edge // 4, dom % 2


def place(x, y, z_hi, z_lo, core):
    return ((z_hi * 4 + y) * 2 + core) * N_EDGE + z_lo * 4 + x


def turn(v):
    x, y, z_hi, z_lo, core = coords(v)
    return place(x, z_lo % 4, z_hi, y + 4 * core, z_lo // 4)


def ahead(v):
    dom, edge = v // N_EDGE, v % N_EDGE
    return turn((dom + 1) % N_DOM * N_EDGE + edge)


ALL = range(N_DOM * N_EDGE)
TURN = [(v, turn(v)) for v in ALL]
AHEAD = [(v, ahead(v)) for v in ALL]
BACK = [(ahead(v), v) for v in ALL]
NEXT = [(turn(v), ahead(v)) for v in ALL]


OTHER = []
for v in ALL:
    x, y, z_hi, z_lo, core = coords(v)
    OTHER.append((v, place(x, y, z_hi, z_lo, 1 - core)))

PLANES = [[place(c % 4, c // 4 % 4, z // 8, z % 8, c // 16) for c in range(32)] for z in range(16)]
SHEETS = [plane[16 * core : 16 * core + 16] for plane in PLANES for core in range(2)]


def z_pairs(step):
    pairs = []
    for v in ALL:
        x, y, z_hi, z_lo, core = coords(v)
        z = (z_hi * 8 + z_lo) ^ step
        pairs.append((v, place(x, y, z // 8, z % 8, core)))
    return pairs


def send(value, pairs):
    return lax.ppermute(value, AXES, pairs)


def exchange(value, groups):
    return lax.all_to_all(value, AXES, 0, 0, axis_index_groups=groups, tiled=True)


def gather_sheet(own):
    return exchange(jnp.broadcast_to(own, (16,) + own.shape), SHEETS)


def together(*values):
    return lax.optimization_barrier(values)


def nt(a, b):
    return lax.dot_general(a, b, (((1,), (1,)), ((), ())), preferred_element_type=F32)


def nn(a, b):
    return jnp.dot(a, b, preferred_element_type=F32)


def blocks_kernel(
    joint, scal, here, lists, own, rel, half, other, mine_out, theirs_out, lhs_out, rel_out, table, acc, rel_acc, sems
):
    slots = 10
    width, block = own.shape
    mid = width // 2
    copies = [
        pltpu.make_async_copy(src, table.at[pl.ds(16 * i, 16)], sems.at[i])
        for i, src in enumerate((half, other))
    ]
    for copy in copies:
        copy.start()

    def clear(k, carry):
        acc[k] = jnp.zeros((width, block), F32)
        return carry

    lax.fori_loop(0, 32, clear, 0)
    rel_acc[...] = jnp.zeros(rel_acc.shape, F32)
    lhs_out[...] = jnp.zeros(lhs_out.shape, F32)
    for copy in copies:
        copy.wait()

    def near(b):
        return ((b >> 4) ^ here[0]) * 16 + (b & 15)

    rows = lax.broadcasted_iota(jnp.int32, (block, block), 0)
    lanes = lax.broadcasted_iota(jnp.int32, (block, block), 1)

    def step(j, carry):
        src_hot = jnp.where(rows == lists[pl.ds(j, 1), :], 1.0, 0.0).astype(BF16)
        tgt_hot = jnp.where(rows == lists[pl.ds(slots + j, 1), :], 1.0, 0.0).astype(BF16)
        dst, rel_id = near(scal[j]), scal[slots + j] * DIGIT + scal[2 * slots + j]
        negs = [near(scal[3 * slots + 4 * j + i]) for i in range(4)]
        rel_tile = pl.ds(pl.multiple_of((rel_id >> 7) * 128, 128), 128)
        rel_row = jnp.where(rows == (rel_id & 127), 1.0, 0.0).astype(BF16)
        rel_lane = jnp.where(lanes == (rel_id & 127), 1.0, 0.0).astype(BF16)
        heads = nn(own[...], src_hot)
        tails = nn(table[dst], tgt_hot)
        rel_value = rel[:, rel_tile]
        high = rel_value.astype(BF16)
        low = (rel_value - high.astype(F32)).astype(BF16)
        op = nn(high, rel_row) + nn(low, rel_row)
        h_re, h_im = heads[:mid], heads[mid:]
        r_re, r_im = op[:mid], op[mid:]
        query = jnp.concatenate([h_re * r_re - h_im * r_im, h_re * r_im + h_im * r_re], 0).astype(BF16)
        query_f = query.astype(F32)
        positive = jnp.sum(query_f * tails, 0, keepdims=True)
        neg_rows = jnp.concatenate([table[n] for n in negs], 1)
        scores = nn(query_f.T.astype(BF16), neg_rows)
        pos_weight = -jax.nn.sigmoid(-positive)
        neg_weight = (jax.nn.sigmoid(scores) * (1.0 / scores.shape[1])).astype(BF16)
        grad_query = pos_weight * tails + nt(neg_rows, neg_weight)
        neg_add = nn(query, neg_weight)
        for i, n in enumerate(negs):
            acc[n] += neg_add[:, block * i : block * (i + 1)]
        acc[dst] += nt((pos_weight * query_f).astype(BF16), tgt_hot)
        g_re, g_im = grad_query[:mid], grad_query[mid:]
        head_grad = jnp.concatenate([g_re * r_re + g_im * r_im, g_im * r_re - g_re * r_im], 0)
        lhs_out[...] += nt(head_grad.astype(BF16), src_hot)
        op_grad = jnp.concatenate([g_re * h_re + g_im * h_im, g_im * h_re - g_re * h_im], 0)
        rel_acc[:, rel_tile] += nn(op_grad.astype(BF16), rel_lane)
        return carry

    lax.fori_loop(0, scal[7 * slots], step, 0)

    tiles = rel_acc.shape[1] // block
    for t in range(tiles - 1):
        rel_out[width * t : width * (t + 1)] = rel_acc[:, block * t : block * (t + 1)].astype(BF16)
    tail = rel_acc[:, block * (tiles - 1) :]
    folded = tail[:FOLD]
    for q in range(1, 4):
        part = tail[FOLD * q : FOLD * (q + 1)]
        if part.shape[0] < FOLD:
            part = jnp.concatenate([part, jnp.zeros((FOLD - part.shape[0], block), F32)], 0)
        folded = folded + pltpu.roll(part, q * block // 4, 1)
    first = width * (tiles - 1)
    rel_out[first : first + FOLD] = folded.astype(BF16)
    rel_out[first + FOLD :] = jnp.zeros((rel_out.shape[0] - first - FOLD, block), BF16)

    def pack(k, carry):
        for side, out in enumerate((mine_out, theirs_out)):
            out[k, :width] = acc[16 * side + k].astype(BF16)
            if joint:
                piece = ((here[0] ^ side) * 16 + k) * PIECE
                out[k, width:] = rel_out[pl.ds(pl.multiple_of(piece, 16), PIECE), :]
        return carry

    lax.fori_loop(0, 16, pack, 0)


def run_blocks(lists, here, own, rel, half, other, joint):
    width, block = own.shape
    rel_lanes = rel.shape[1]
    rows = width + PIECE if joint else width
    vmem = pl.BlockSpec(memory_space=pltpu.VMEM)
    smem = pl.BlockSpec(memory_space=pltpu.SMEM)
    hbm = pl.BlockSpec(memory_space=pl.ANY)
    out_shape = [
        jax.ShapeDtypeStruct((16, rows, block), BF16),
        jax.ShapeDtypeStruct((16, rows, block), BF16),
        jax.ShapeDtypeStruct((width, block), F32),
    ]
    packed = (32 * PIECE, block)
    scratch = [
        pltpu.VMEM((32, width, block), BF16),
        pltpu.VMEM((32, width, block), F32),
        pltpu.VMEM((width, rel_lanes), F32),
        pltpu.SemaphoreType.DMA((2,)),
    ]
    if joint:
        scratch = [pltpu.VMEM(packed, BF16)] + scratch
    else:
        out_shape = out_shape + [jax.ShapeDtypeStruct(packed, BF16)]
    return pl.pallas_call(
        functools.partial(blocks_kernel, joint),
        out_shape=out_shape,
        in_specs=[smem, smem, vmem, vmem, vmem, hbm, hbm],
        out_specs=[vmem] * len(out_shape),
        scratch_shapes=scratch,
        compiler_params=pltpu.CompilerParams(vmem_limit_bytes=40 * MIB),
        cost_estimate=pl.CostEstimate(flops=2 * 10**9, bytes_accessed=10**7, transcendentals=10**6),
        name="edge_blocks",
    )(lists[20], here, lists, own, rel, half, other)


def adagrad(grads, kept):
    width = grads.shape[0]
    state = kept[width : width + 1] + jnp.sum(grads * grads, 0, keepdims=True) * (1.0 / width)
    weights = kept[:width] - grads * (ENT_RATE / jnp.sqrt(state))
    return weights, state


def add_pieces(pieces):
    def add(k, total):
        return total + pieces[k].astype(F32)

    return lax.fori_loop(1, pieces.shape[0], add, pieces[0].astype(F32))


def middle_kernel(pieces, lhs, kept, kept_out, table_out, rel_out):
    width = lhs.shape[0]
    total = add_pieces(pieces)
    weights, state = adagrad(lhs[...] + total[:width], kept[...])
    kept_out[:width] = weights
    kept_out[width:] = jnp.broadcast_to(state, (kept.shape[0] - width, state.shape[1]))
    table_out[...] = weights.astype(BF16)
    rel_out[...] = total[width:]


def middle(pieces, lhs, kept):
    return pl.pallas_call(
        middle_kernel,
        out_shape=(
            jax.ShapeDtypeStruct(kept.shape, F32),
            jax.ShapeDtypeStruct(lhs.shape, BF16),
            jax.ShapeDtypeStruct((PIECE, lhs.shape[1]), F32),
        ),
        compiler_params=pltpu.CompilerParams(vmem_limit_bytes=16 * MIB),
        name="middle_update",
    )(pieces, lhs, kept)


def fold_kernel(pieces, out):
    out[...] = add_pieces(pieces).astype(out.dtype)


def fold(pieces, kind):
    return pl.pallas_call(
        fold_kernel,
        out_shape=jax.ShapeDtypeStruct(pieces.shape[1:], kind),
        compiler_params=pltpu.CompilerParams(vmem_limit_bytes=16 * MIB),
        name="fold_pieces",
    )(pieces)


def last_kernel(rhs, lhs, kept, weights_out, state_out):
    weights, state = adagrad(rhs[...].astype(F32) + lhs[...].astype(F32), kept[...])
    weights_out[...] = weights
    state_out[...] = state


def last(rhs, lhs, kept):
    width, block = lhs.shape
    return pl.pallas_call(
        last_kernel,
        out_shape=(
            jax.ShapeDtypeStruct((width, block), F32),
            jax.ShapeDtypeStruct((1, block), F32),
        ),
        name="last_update",
    )(rhs, lhs, kept)


def z_step(total, step, kind):
    mine = total.astype(kind)
    return mine.astype(F32) + send(mine, z_pairs(step)).astype(F32)


def z_steps(total):
    for step, kind in ((1, F32), (2, F32), (4, BF16)):
        total = z_step(total, step, kind)
    return total


def spread_relations(mine):
    mine = mine.astype(BF16)
    return exchange(jnp.broadcast_to(mine, (32,) + mine.shape), PLANES)


def relation_kernel(packed, rel, rel_state, rel_out, state_out):
    width, count = rel_state.shape
    block = packed.shape[1]
    tiles = -(-count // block)
    rest = count - block * (tiles - 1)

    def update(grads, rows, lanes):
        state = rel_state[rows, lanes] + grads * grads
        state_out[rows, lanes] = state
        rel_out[rows, lanes] = rel[rows, lanes] - REL_RATE * grads / jnp.sqrt(state)

    def full(p, carry):
        for t in range(tiles - 1):
            grads = packed[pl.ds(pl.multiple_of(width * t + p * GROUP, GROUP), GROUP), :].astype(F32)
            rows = pl.ds(pl.multiple_of(p * GROUP, GROUP), GROUP)
            update(grads, rows, slice(block * t, block * (t + 1)))
        return carry

    lax.fori_loop(0, width // GROUP, full, 0)
    first = width * (tiles - 1)
    folded = packed[first : first + FOLD, :].astype(F32)
    for q in range(4):
        stop = min(FOLD * (q + 1), width)
        grads = folded if q == 0 else pltpu.roll(folded, block - q * block // 4, 1)
        lanes = slice(block * (tiles - 1), count)
        update(grads[: stop - FOLD * q, :rest], slice(FOLD * q, stop), lanes)
    if rel_out.shape[1] > count:
        rel_out[:, count:] = jnp.zeros((width, rel_out.shape[1] - count), F32)


def relation_update(pieces, rel, rel_state, lanes):
    width = rel.shape[0]
    return pl.pallas_call(
        relation_kernel,
        out_shape=(
            jax.ShapeDtypeStruct((width, lanes), F32),
            jax.ShapeDtypeStruct(rel_state.shape, F32),
        ),
        compiler_params=pltpu.CompilerParams(vmem_limit_bytes=16 * MIB),
        name="relation_update",
    )(pieces.reshape(-1, pieces.shape[2]), rel, rel_state)


def shards(
    entities,
    entity_state,
    relations,
    relation_state,
    live_blocks,
    dst_blocks,
    relation_ids,
    source_rows,
    target_rows,
    negative_blocks,
):
    block, width = entities.shape
    dom = lax.axis_index("dom")
    here = (dom % 2).astype(jnp.int32)[None]

    def lists_of(r):
        ids = relation_ids[r]
        numbers = [dst_blocks[r], ids // DIGIT, ids % DIGIT, negative_blocks[r].reshape(-1), live_blocks[r]]
        numbers = jnp.concatenate(numbers)
        numbers = jnp.pad(numbers, (0, block - numbers.shape[0]))[None]
        rows = jnp.concatenate([source_rows[r], target_rows[r], numbers])
        return jnp.pad(rows, ((0, LISTS - rows.shape[0]), (0, 0))).astype(BF16)

    weights = entities.T
    own = send(weights.astype(BF16), TURN)
    own, weights, source_rows, target_rows, dst_blocks = together(
        own, weights, source_rows, target_rows, dst_blocks
    )
    lists = send(jnp.concatenate([lists_of(0), lists_of(1)]), TURN)
    kept = send(jnp.concatenate([weights, jnp.broadcast_to(entity_state[None], (8, block))]), TURN)

    count = relations.shape[0]
    lanes = -(-count // block) * block
    rel = jnp.pad(relations.T, ((0, 0), (0, lanes - count)))
    rel_state = relation_state.T

    half, lists, kept = together(gather_sheet(own), lists, kept)
    other = send(half, OTHER)
    now = lists[:LISTS].astype(jnp.int32)
    mine, theirs, lhs = run_blocks(now, here, own, rel, half, other, True)
    pieces = exchange(mine + send(theirs, OTHER), SHEETS)
    kept, own, rel_mine = middle(pieces, lhs, kept)
    source = send(jnp.concatenate([own, lists[LISTS:]]), NEXT)
    kept = send(kept, TURN)
    half, source, rel_mine = together(gather_sheet(own), source, z_steps(rel_mine))
    other = send(half, OTHER)
    rel_sum = spread_relations(z_step(rel_mine, 8, BF16))
    rel, rel_state = relation_update(rel_sum, rel, rel_state, lanes)
    other, kept = together(other, kept)

    now = source[width:].astype(jnp.int32)
    mine, theirs, lhs, rel_part = run_blocks(now, here, source[:width], rel, half, other, False)
    summed, lhs = together(mine + send(theirs, OTHER), lhs.astype(BF16))
    lhs = send(lhs, BACK)
    rel_pieces = exchange(rel_part.reshape(32, PIECE, block), PLANES)
    summed, rel_pieces, lhs = together(summed, rel_pieces, lhs)
    rel_mine = z_steps(fold(rel_pieces, F32))
    rhs = send(fold(exchange(summed, SHEETS), BF16), TURN)
    rel_sum = spread_relations(z_step(rel_mine, 8, BF16))
    weights, state = last(rhs, lhs, kept)
    rel, rel_state = relation_update(rel_sum, rel, rel_state, count)
    return (weights.T, state[0], rel.T, rel_state.T)


def solution(mesh):
    placed = (
        P(AXES, None),
        P(AXES),
        P(),
        P(),
        P(None, AXES),
        P(None, AXES),
        P(None, AXES),
        P(None, AXES, None),
        P(None, AXES, None),
        P(None, AXES, None),
    )
    return jax.shard_map(
        shards,
        mesh=mesh,
        in_specs=placed,
        out_specs=(P(AXES, None), P(AXES), P(), P()),
        check_vma=False,
    )
```

```python
import jax
import jax.numpy as jnp
from jax import lax
from jax.experimental import pallas as pl
from jax.experimental.pallas import tpu as pltpu
from jax.sharding import PartitionSpec as P

AXES = ("dom", "edge")
N_DOM, N_EDGE = 16, 32
ENT_RATE = 0.25
REL_RATE = 0.25
F32, BF16 = jnp.float32, jnp.bfloat16
GROUP = 16
PIECE = 80
FOLD = 112
DIGIT = 32
LISTS = 32
MIB = 1024 * 1024


def coords(v):
    dom, edge = v // N_EDGE, v % N_EDGE
    return edge % 4, (dom // 2) % 4, dom // 8, edge // 4, dom % 2


def place(x, y, z_hi, z_lo, core):
    return ((z_hi * 4 + y) * 2 + core) * N_EDGE + z_lo * 4 + x


def turn(v):
    x, y, z_hi, z_lo, core = coords(v)
    return place(x, z_lo % 4, z_hi, y + 4 * core, z_lo // 4)


def ahead(v):
    dom, edge = v // N_EDGE, v % N_EDGE
    return turn((dom + 1) % N_DOM * N_EDGE + edge)


ALL = range(N_DOM * N_EDGE)
TURN = [(v, turn(v)) for v in ALL]
NEXT = [(turn(v), ahead(v)) for v in ALL]
PREVIOUS = [(target, source) for source, target in NEXT]


OTHER = []
for v in ALL:
    x, y, z_hi, z_lo, core = coords(v)
    OTHER.append((v, place(x, y, z_hi, z_lo, 1 - core)))

PLANES = [[place(c % 4, c // 4 % 4, z // 8, z % 8, c // 16) for c in range(32)] for z in range(16)]
SHEETS = [plane[16 * core : 16 * core + 16] for plane in PLANES for core in range(2)]


def z_pairs(step):
    pairs = []
    for v in ALL:
        x, y, z_hi, z_lo, core = coords(v)
        z = (z_hi * 8 + z_lo) ^ step
        pairs.append((v, place(x, y, z // 8, z % 8, core)))
    return pairs


def send(value, pairs):
    return lax.ppermute(value, AXES, pairs)


def exchange(value, groups):
    return lax.all_to_all(value, AXES, 0, 0, axis_index_groups=groups, tiled=True)


def gather_sheet(own):
    return exchange(jnp.broadcast_to(own, (16,) + own.shape), SHEETS)


def together(*values):
    return lax.optimization_barrier(values)


def nt(a, b):
    return lax.dot_general(a, b, (((1,), (1,)), ((), ())), preferred_element_type=F32)


def nn(a, b):
    return jnp.dot(a, b, preferred_element_type=F32)


def blocks_kernel(
    scal, here, lists, own, rel, half, other, mine_out, theirs_out, lhs_out, rel_out, table, acc, rel_acc, sems
):
    slots = 10
    width, block = own.shape
    mid = width // 2
    copies = [
        pltpu.make_async_copy(src, table.at[pl.ds(16 * i, 16)], sems.at[i])
        for i, src in enumerate((half, other))
    ]
    for copy in copies:
        copy.start()

    def clear(k, carry):
        acc[k] = jnp.zeros((width, block), F32)
        return carry

    lax.fori_loop(0, 32, clear, 0)
    rel_acc[...] = jnp.zeros(rel_acc.shape, F32)
    lhs_out[...] = jnp.zeros(lhs_out.shape, F32)
    for copy in copies:
        copy.wait()

    def near(b):
        return ((b >> 4) ^ here[0]) * 16 + (b & 15)

    rows = lax.broadcasted_iota(jnp.int32, (block, block), 0)
    lanes = lax.broadcasted_iota(jnp.int32, (block, block), 1)

    def step(j, carry):
        src_hot = jnp.where(rows == lists[pl.ds(j, 1), :], 1.0, 0.0).astype(BF16)
        tgt_hot = jnp.where(rows == lists[pl.ds(slots + j, 1), :], 1.0, 0.0).astype(BF16)
        dst, rel_id = near(scal[j]), scal[slots + j] * DIGIT + scal[2 * slots + j]
        negs = [near(scal[3 * slots + 4 * j + i]) for i in range(4)]
        rel_tile = pl.ds(pl.multiple_of((rel_id >> 7) * 128, 128), 128)
        rel_row = jnp.where(rows == (rel_id & 127), 1.0, 0.0).astype(BF16)
        rel_lane = jnp.where(lanes == (rel_id & 127), 1.0, 0.0).astype(BF16)
        heads = nn(own[...], src_hot)
        tails = nn(table[dst], tgt_hot)
        rel_value = rel[:, rel_tile]
        high = rel_value.astype(BF16)
        low = (rel_value - high.astype(F32)).astype(BF16)
        op = nn(high, rel_row) + nn(low, rel_row)
        h_re, h_im = heads[:mid], heads[mid:]
        r_re, r_im = op[:mid], op[mid:]
        query = jnp.concatenate([h_re * r_re - h_im * r_im, h_re * r_im + h_im * r_re], 0).astype(BF16)
        query_f = query.astype(F32)
        positive = jnp.sum(query_f * tails, 0, keepdims=True)
        neg_rows = jnp.concatenate([table[n] for n in negs], 1)
        scores = nn(query_f.T.astype(BF16), neg_rows)
        pos_weight = -jax.nn.sigmoid(-positive)
        neg_weight = (jax.nn.sigmoid(scores) * (1.0 / scores.shape[1])).astype(BF16)
        grad_query = pos_weight * tails + nt(neg_rows, neg_weight)
        neg_add = nn(query, neg_weight)
        for i, n in enumerate(negs):
            acc[n] += neg_add[:, block * i : block * (i + 1)]
        acc[dst] += nt((pos_weight * query_f).astype(BF16), tgt_hot)
        g_re, g_im = grad_query[:mid], grad_query[mid:]
        head_grad = jnp.concatenate([g_re * r_re + g_im * r_im, g_im * r_re - g_re * r_im], 0)
        lhs_out[...] += nt(head_grad.astype(BF16), src_hot)
        op_grad = jnp.concatenate([g_re * h_re + g_im * h_im, g_im * h_re - g_re * h_im], 0)
        rel_acc[:, rel_tile] += nn(op_grad.astype(BF16), rel_lane)
        return carry

    lax.fori_loop(0, scal[7 * slots], step, 0)

    def pack(k, carry):
        mine_out[k] = acc[k].astype(BF16)
        theirs_out[k] = acc[16 + k].astype(BF16)
        return carry

    lax.fori_loop(0, 16, pack, 0)
    tiles = rel_acc.shape[1] // block
    for t in range(tiles - 1):
        rel_out[width * t : width * (t + 1)] = rel_acc[:, block * t : block * (t + 1)].astype(BF16)
    tail = rel_acc[:, block * (tiles - 1) :]
    folded = tail[:FOLD]
    for q in range(1, 4):
        part = tail[FOLD * q : FOLD * (q + 1)]
        if part.shape[0] < FOLD:
            part = jnp.concatenate([part, jnp.zeros((FOLD - part.shape[0], block), F32)], 0)
        folded = folded + pltpu.roll(part, q * block // 4, 1)
    first = width * (tiles - 1)
    rel_out[first : first + FOLD] = folded.astype(BF16)
    rel_out[first + FOLD :] = jnp.zeros((rel_out.shape[0] - first - FOLD, block), BF16)


def run_blocks(lists, here, own, rel, half, other):
    width, block = own.shape
    rel_lanes = rel.shape[1]
    vmem = pl.BlockSpec(memory_space=pltpu.VMEM)
    smem = pl.BlockSpec(memory_space=pltpu.SMEM)
    hbm = pl.BlockSpec(memory_space=pl.ANY)
    return pl.pallas_call(
        blocks_kernel,
        out_shape=(
            jax.ShapeDtypeStruct((16, width, block), BF16),
            jax.ShapeDtypeStruct((16, width, block), BF16),
            jax.ShapeDtypeStruct((width, block), F32),
            jax.ShapeDtypeStruct((32 * PIECE, block), BF16),
        ),
        in_specs=[smem, smem, vmem, vmem, vmem, hbm, hbm],
        out_specs=(vmem, vmem, vmem, vmem),
        scratch_shapes=[
            pltpu.VMEM((32, width, block), BF16),
            pltpu.VMEM((32, width, block), F32),
            pltpu.VMEM((width, rel_lanes), F32),
            pltpu.SemaphoreType.DMA((2,)),
        ],
        compiler_params=pltpu.CompilerParams(vmem_limit_bytes=40 * MIB),
        cost_estimate=pl.CostEstimate(flops=2 * 10**9, bytes_accessed=10**7, transcendentals=10**6),
        name="edge_blocks",
    )(lists[20], here, lists, own, rel, half, other)


def adagrad(grads, kept):
    width = grads.shape[0]
    state = kept[width : width + 1] + jnp.sum(grads * grads, 0, keepdims=True) * (1.0 / width)
    weights = kept[:width] - grads * (ENT_RATE / jnp.sqrt(state))
    return weights, state


def add_pieces(pieces):
    def add(k, total):
        return total + pieces[k].astype(F32)

    return lax.fori_loop(1, pieces.shape[0], add, pieces[0].astype(F32))


def middle_kernel(pieces, lhs, kept, kept_out, table_out):
    width = lhs.shape[0]
    weights, state = adagrad(lhs[...] + add_pieces(pieces), kept[...])
    kept_out[:width] = weights
    kept_out[width:] = jnp.broadcast_to(state, (kept.shape[0] - width, state.shape[1]))
    table_out[...] = weights.astype(BF16)


def middle(pieces, lhs, kept):
    return pl.pallas_call(
        middle_kernel,
        out_shape=(jax.ShapeDtypeStruct(kept.shape, F32), jax.ShapeDtypeStruct(lhs.shape, BF16)),
        compiler_params=pltpu.CompilerParams(vmem_limit_bytes=16 * MIB),
        name="middle_update",
    )(pieces, lhs, kept)


def fold_kernel(pieces, more, out):
    out[...] = (add_pieces(pieces) + more[...].astype(F32)).astype(out.dtype)


def fold(pieces, more):
    return pl.pallas_call(
        fold_kernel,
        out_shape=jax.ShapeDtypeStruct(more.shape, more.dtype),
        compiler_params=pltpu.CompilerParams(vmem_limit_bytes=16 * MIB),
        name="fold_pieces",
    )(pieces, more)


def last_kernel(grads, kept, weights_out, state_out):
    weights, state = adagrad(grads[...].astype(F32), kept[...])
    weights_out[...] = weights
    state_out[...] = state


def last(grads, kept):
    width, block = grads.shape
    return pl.pallas_call(
        last_kernel,
        out_shape=(
            jax.ShapeDtypeStruct((width, block), F32),
            jax.ShapeDtypeStruct((1, block), F32),
        ),
        name="last_update",
    )(grads, kept)


def z_step(total, step, kind):
    mine = total.astype(kind)
    return mine.astype(F32) + send(mine, z_pairs(step)).astype(F32)


def z_steps(total):
    total = jnp.sum(total, 0, dtype=F32)
    for step, kind in ((1, F32), (2, F32), (4, BF16)):
        total = z_step(total, step, kind)
    return total


def spread_relations(mine):
    mine = mine.astype(BF16)
    return exchange(jnp.broadcast_to(mine, (32,) + mine.shape), PLANES)


def relation_kernel(packed, rel, rel_state, rel_out, state_out):
    width, count = rel_state.shape
    block = packed.shape[1]
    tiles = -(-count // block)
    rest = count - block * (tiles - 1)

    def update(grads, rows, lanes):
        state = rel_state[rows, lanes] + grads * grads
        state_out[rows, lanes] = state
        rel_out[rows, lanes] = rel[rows, lanes] - REL_RATE * grads / jnp.sqrt(state)

    def full(p, carry):
        for t in range(tiles - 1):
            grads = packed[pl.ds(pl.multiple_of(width * t + p * GROUP, GROUP), GROUP), :].astype(F32)
            rows = pl.ds(pl.multiple_of(p * GROUP, GROUP), GROUP)
            update(grads, rows, slice(block * t, block * (t + 1)))
        return carry

    lax.fori_loop(0, width // GROUP, full, 0)
    first = width * (tiles - 1)
    folded = packed[first : first + FOLD, :].astype(F32)
    for q in range(4):
        stop = min(FOLD * (q + 1), width)
        grads = folded if q == 0 else pltpu.roll(folded, block - q * block // 4, 1)
        lanes = slice(block * (tiles - 1), count)
        update(grads[: stop - FOLD * q, :rest], slice(FOLD * q, stop), lanes)
    if rel_out.shape[1] > count:
        rel_out[:, count:] = jnp.zeros((width, rel_out.shape[1] - count), F32)


def relation_update(pieces, rel, rel_state, lanes):
    width = rel.shape[0]
    return pl.pallas_call(
        relation_kernel,
        out_shape=(
            jax.ShapeDtypeStruct((width, lanes), F32),
            jax.ShapeDtypeStruct(rel_state.shape, F32),
        ),
        compiler_params=pltpu.CompilerParams(vmem_limit_bytes=16 * MIB),
        name="relation_update",
    )(pieces.reshape(-1, pieces.shape[2]), rel, rel_state)


def shards(
    entities,
    entity_state,
    relations,
    relation_state,
    live_blocks,
    dst_blocks,
    relation_ids,
    source_rows,
    target_rows,
    negative_blocks,
):
    block, width = entities.shape
    dom = lax.axis_index("dom")
    here = (dom % 2).astype(jnp.int32)[None]

    def lists_of(r):
        ids = relation_ids[r]
        numbers = [dst_blocks[r], ids // DIGIT, ids % DIGIT, negative_blocks[r].reshape(-1), live_blocks[r]]
        numbers = jnp.concatenate(numbers)
        numbers = jnp.pad(numbers, (0, block - numbers.shape[0]))[None]
        rows = jnp.concatenate([source_rows[r], target_rows[r], numbers])
        return jnp.pad(rows, ((0, LISTS - rows.shape[0]), (0, 0))).astype(BF16)

    weights = entities.T
    own = send(weights.astype(BF16), TURN)
    own, weights, source_rows, target_rows, dst_blocks = together(
        own, weights, source_rows, target_rows, dst_blocks
    )
    lists = send(jnp.concatenate([lists_of(0), lists_of(1)]), TURN)
    kept = send(jnp.concatenate([weights, jnp.broadcast_to(entity_state[None], (8, block))]), TURN)

    count = relations.shape[0]
    lanes = -(-count // block) * block
    rel = jnp.pad(relations.T, ((0, 0), (0, lanes - count)))
    rel_state = relation_state.T

    half, lists, kept = together(gather_sheet(own), lists, kept)
    other = send(half, OTHER)
    now = lists[:LISTS].astype(jnp.int32)
    mine, theirs, lhs, rel_part = run_blocks(now, here, own, rel, half, other)
    rel_pieces = exchange(rel_part.reshape(32, PIECE, block), PLANES)
    summed, rel_pieces = together(mine + send(theirs, OTHER), rel_pieces)
    pieces, rel_mine = together(exchange(summed, SHEETS), z_steps(rel_pieces))
    kept, own = middle(pieces, lhs, kept)
    source = send(jnp.concatenate([own, lists[LISTS:]]), NEXT)
    kept = send(kept, TURN)
    half, source, rel_mine = together(gather_sheet(own), source, z_step(rel_mine, 8, BF16))
    other = send(half, OTHER)
    rel, rel_state = relation_update(spread_relations(rel_mine), rel, rel_state, lanes)
    other, kept = together(other, kept)

    now = source[width:].astype(jnp.int32)
    mine, theirs, lhs, rel_part = run_blocks(now, here, source[:width], rel, half, other)
    rel_pieces = exchange(rel_part.reshape(32, PIECE, block), PLANES)
    summed, lhs = together(mine + send(theirs, OTHER), lhs.astype(BF16))
    summed, rel_pieces, lhs = together(summed, rel_pieces, send(lhs, PREVIOUS))
    rel_mine = z_step(z_steps(rel_pieces), 8, BF16)
    pieces, rel_mine = together(exchange(summed, SHEETS), rel_mine)
    grads = send(fold(pieces, lhs), TURN)
    rel_sum = spread_relations(rel_mine)
    weights, state = last(grads, kept)
    rel, rel_state = relation_update(rel_sum, rel, rel_state, count)
    return (weights.T, state[0], rel.T, rel_state.T)


def solution(mesh):
    placed = (
        P(AXES, None),
        P(AXES),
        P(),
        P(),
        P(None, AXES),
        P(None, AXES),
        P(None, AXES),
        P(None, AXES, None),
        P(None, AXES, None),
        P(None, AXES, None),
    )
    return jax.shard_map(
        shards,
        mesh=mesh,
        in_specs=placed,
        out_specs=(P(AXES, None), P(AXES), P(), P()),
        check_vma=False,
    )
```

```python
import jax
import jax.numpy as jnp
from jax import lax
from jax.experimental import pallas as pl
from jax.experimental.pallas import tpu as pltpu
from jax.sharding import PartitionSpec as P

AXES = ("dom", "edge")
N_DOM, N_EDGE = 16, 32
ENT_RATE = 0.25
REL_RATE = 0.25
F32, BF16 = jnp.float32, jnp.bfloat16
GROUP = 16
PIECE = 80
FOLD = 112
DIGIT = 32
LISTS = 32
MIB = 1024 * 1024


def coords(v):
    dom, edge = v // N_EDGE, v % N_EDGE
    return edge % 4, (dom // 2) % 4, dom // 8, edge // 4, dom % 2


def place(x, y, z_hi, z_lo, core):
    return ((z_hi * 4 + y) * 2 + core) * N_EDGE + z_lo * 4 + x


def turn(v):
    x, y, z_hi, z_lo, core = coords(v)
    return place(x, z_lo % 4, z_hi, y + 4 * core, z_lo // 4)


def ahead(v):
    dom, edge = v // N_EDGE, v % N_EDGE
    return turn((dom + 1) % N_DOM * N_EDGE + edge)


ALL = range(N_DOM * N_EDGE)
TURN = [(v, turn(v)) for v in ALL]
NEXT = [(turn(v), ahead(v)) for v in ALL]
PREVIOUS = [(target, source) for source, target in NEXT]


OTHER = []
for v in ALL:
    x, y, z_hi, z_lo, core = coords(v)
    OTHER.append((v, place(x, y, z_hi, z_lo, 1 - core)))

PLANES = [[place(c % 4, c // 4 % 4, z // 8, z % 8, c // 16) for c in range(32)] for z in range(16)]
SHEETS = [plane[16 * core : 16 * core + 16] for plane in PLANES for core in range(2)]


def z_pairs(step):
    pairs = []
    for v in ALL:
        x, y, z_hi, z_lo, core = coords(v)
        z = (z_hi * 8 + z_lo) ^ step
        pairs.append((v, place(x, y, z // 8, z % 8, core)))
    return pairs


def send(value, pairs):
    return lax.ppermute(value, AXES, pairs)


def exchange(value, groups):
    return lax.all_to_all(value, AXES, 0, 0, axis_index_groups=groups, tiled=True)


def gather_sheet(own):
    return exchange(jnp.broadcast_to(own, (16,) + own.shape), SHEETS)


def together(*values):
    return lax.optimization_barrier(values)


def nt(a, b):
    return lax.dot_general(a, b, (((1,), (1,)), ((), ())), preferred_element_type=F32)


def nn(a, b):
    return jnp.dot(a, b, preferred_element_type=F32)


def blocks_kernel(
    scal, here, lists, own, rel, half, other, mine_out, theirs_out, lhs_out, rel_out, table, acc, rel_acc, sems
):
    slots = 10
    width, block = own.shape
    mid = width // 2
    copies = [
        pltpu.make_async_copy(src, table.at[pl.ds(16 * i, 16)], sems.at[i])
        for i, src in enumerate((half, other))
    ]
    for copy in copies:
        copy.start()

    def clear(k, carry):
        acc[k] = jnp.zeros((width, block), F32)
        return carry

    lax.fori_loop(0, 32, clear, 0)
    rel_acc[...] = jnp.zeros(rel_acc.shape, F32)
    lhs_out[...] = jnp.zeros(lhs_out.shape, F32)
    for copy in copies:
        copy.wait()

    def near(b):
        return ((b >> 4) ^ here[0]) * 16 + (b & 15)

    both = 2 * block
    rows = lax.broadcasted_iota(jnp.int32, (both, both), 0)
    lanes = lax.broadcasted_iota(jnp.int32, (both, both), 1)
    count = scal[7 * slots]

    def hot(match):
        return jnp.where(match, 1.0, 0.0).astype(BF16)

    def step(i, carry):
        pair = (2 * i, 2 * i + 1)
        live = (1.0, jnp.where(pair[1] < count, 1.0, 0.0))
        sources = jnp.concatenate([lists[pl.ds(j, 1), :] for j in pair], 1)
        targets = jnp.concatenate([lists[pl.ds(slots + j, 1), :] + block * s for s, j in enumerate(pair)], 1)
        src_hot = hot(rows[:block] == sources)
        tgt_hot = hot(rows == targets)
        dsts = [near(scal[j]) for j in pair]
        rel_ids = [scal[slots + j] * DIGIT + scal[2 * slots + j] for j in pair]
        rel_lanes = [rel_id & (block - 1) for rel_id in rel_ids]
        rel_tiles = [pl.ds(pl.multiple_of((rel_id >> 7) * block, block), block) for rel_id in rel_ids]
        rel_hot = hot(lanes == jnp.where(rows < block, rel_lanes[0], rel_lanes[1] + block))
        heads = nn(own[...], src_hot)
        tails = nn(jnp.concatenate([table[dst] for dst in dsts], 1), tgt_hot)
        columns = [
            pltpu.roll(rel[:, tile], (block - lane) & (block - 1), 1)[:, :1]
            for tile, lane in zip(rel_tiles, rel_lanes)
        ]
        op = jnp.concatenate([jnp.broadcast_to(column, (width, block)) for column in columns], 1)
        h_re, h_im = heads[:mid], heads[mid:]
        r_re, r_im = op[:mid], op[mid:]
        query = jnp.concatenate([h_re * r_re - h_im * r_im, h_re * r_im + h_im * r_re], 0).astype(BF16)
        query_f = query.astype(F32)
        query_t = query_f.T.astype(BF16)
        positive = jnp.sum(query_f * tails, 0, keepdims=True)
        live_lanes = jnp.where(lanes[:1] < block, live[0], live[1])
        pos_weight = -jax.nn.sigmoid(-positive) * live_lanes
        neg_grads = []
        for s, j in enumerate(pair):
            negs = [near(scal[3 * slots + 4 * j + n]) for n in range(4)]
            neg_rows = jnp.concatenate([table[n] for n in negs], 1)
            scores = nn(query_t[block * s : block * (s + 1)], neg_rows)
            neg_weight = (jax.nn.sigmoid(scores) * (live[s] / scores.shape[1])).astype(BF16)
            neg_grads.append(nt(neg_rows, neg_weight))
            neg_add = nn(query[:, block * s : block * (s + 1)], neg_weight)
            for t, n in enumerate(negs):
                acc[n] += neg_add[:, block * t : block * (t + 1)]
        grad_query = pos_weight * tails + jnp.concatenate(neg_grads, 1)
        tgt_add = nt((pos_weight * query_f).astype(BF16), tgt_hot)
        g_re, g_im = grad_query[:mid], grad_query[mid:]
        head_grad = jnp.concatenate([g_re * r_re + g_im * r_im, g_im * r_re - g_re * r_im], 0)
        lhs_out[...] += nt(head_grad.astype(BF16), src_hot)
        op_grad = jnp.concatenate([g_re * h_re + g_im * h_im, g_im * h_re - g_re * h_im], 0)
        rel_add = nn(op_grad.astype(BF16), rel_hot)
        for s in range(2):
            acc[dsts[s]] += tgt_add[:, block * s : block * (s + 1)]
            rel_acc[:, rel_tiles[s]] += rel_add[:, block * s : block * (s + 1)]
        return carry

    lax.fori_loop(0, (count + 1) >> 1, step, 0)

    def pack(k, carry):
        mine_out[k] = acc[k].astype(BF16)
        theirs_out[k] = acc[16 + k].astype(BF16)
        return carry

    lax.fori_loop(0, 16, pack, 0)
    tiles = rel_acc.shape[1] // block
    for t in range(tiles - 1):
        rel_out[width * t : width * (t + 1)] = rel_acc[:, block * t : block * (t + 1)].astype(BF16)
    tail = rel_acc[:, block * (tiles - 1) :]
    folded = tail[:FOLD]
    for q in range(1, 4):
        part = tail[FOLD * q : FOLD * (q + 1)]
        if part.shape[0] < FOLD:
            part = jnp.concatenate([part, jnp.zeros((FOLD - part.shape[0], block), F32)], 0)
        folded = folded + pltpu.roll(part, q * block // 4, 1)
    first = width * (tiles - 1)
    rel_out[first : first + FOLD] = folded.astype(BF16)
    rel_out[first + FOLD :] = jnp.zeros((rel_out.shape[0] - first - FOLD, block), BF16)


def run_blocks(lists, here, own, rel, half, other):
    width, block = own.shape
    rel_lanes = rel.shape[1]
    vmem = pl.BlockSpec(memory_space=pltpu.VMEM)
    smem = pl.BlockSpec(memory_space=pltpu.SMEM)
    hbm = pl.BlockSpec(memory_space=pl.ANY)
    return pl.pallas_call(
        blocks_kernel,
        out_shape=(
            jax.ShapeDtypeStruct((16, width, block), BF16),
            jax.ShapeDtypeStruct((16, width, block), BF16),
            jax.ShapeDtypeStruct((width, block), F32),
            jax.ShapeDtypeStruct((32 * PIECE, block), BF16),
        ),
        in_specs=[smem, smem, vmem, vmem, vmem, hbm, hbm],
        out_specs=(vmem, vmem, vmem, vmem),
        scratch_shapes=[
            pltpu.VMEM((32, width, block), BF16),
            pltpu.VMEM((32, width, block), F32),
            pltpu.VMEM((width, rel_lanes), F32),
            pltpu.SemaphoreType.DMA((2,)),
        ],
        compiler_params=pltpu.CompilerParams(vmem_limit_bytes=40 * MIB),
        cost_estimate=pl.CostEstimate(flops=2 * 10**9, bytes_accessed=10**7, transcendentals=10**6),
        name="edge_blocks",
    )(lists[20], here, lists, own, rel, half, other)


def adagrad(grads, kept):
    width = grads.shape[0]
    state = kept[width : width + 1] + jnp.sum(grads * grads, 0, keepdims=True) * (1.0 / width)
    weights = kept[:width] - grads * (ENT_RATE / jnp.sqrt(state))
    return weights, state


def add_pieces(pieces):
    def add(k, total):
        return total + pieces[k].astype(F32)

    return lax.fori_loop(1, pieces.shape[0], add, pieces[0].astype(F32))


def middle_kernel(pieces, lhs, kept, kept_out, table_out):
    width = lhs.shape[0]
    weights, state = adagrad(lhs[...] + add_pieces(pieces), kept[...])
    kept_out[:width] = weights
    kept_out[width:] = jnp.broadcast_to(state, (kept.shape[0] - width, state.shape[1]))
    table_out[...] = weights.astype(BF16)


def middle(pieces, lhs, kept):
    return pl.pallas_call(
        middle_kernel,
        out_shape=(jax.ShapeDtypeStruct(kept.shape, F32), jax.ShapeDtypeStruct(lhs.shape, BF16)),
        compiler_params=pltpu.CompilerParams(vmem_limit_bytes=16 * MIB),
        name="middle_update",
    )(pieces, lhs, kept)


def fold_kernel(pieces, more, out):
    out[...] = (add_pieces(pieces) + more[...].astype(F32)).astype(out.dtype)


def fold(pieces, more):
    return pl.pallas_call(
        fold_kernel,
        out_shape=jax.ShapeDtypeStruct(more.shape, more.dtype),
        compiler_params=pltpu.CompilerParams(vmem_limit_bytes=16 * MIB),
        name="fold_pieces",
    )(pieces, more)


def last_kernel(grads, kept, weights_out, state_out):
    weights, state = adagrad(grads[...].astype(F32), kept[...])
    weights_out[...] = weights
    state_out[...] = state


def last(grads, kept):
    width, block = grads.shape
    return pl.pallas_call(
        last_kernel,
        out_shape=(
            jax.ShapeDtypeStruct((width, block), F32),
            jax.ShapeDtypeStruct((1, block), F32),
        ),
        name="last_update",
    )(grads, kept)


def z_step(total, step, kind):
    mine = total.astype(kind)
    return mine.astype(F32) + send(mine, z_pairs(step)).astype(F32)


def z_steps(total):
    total = jnp.sum(total, 0, dtype=F32)
    for step, kind in ((1, F32), (2, F32), (4, BF16)):
        total = z_step(total, step, kind)
    return total


def spread_relations(mine):
    mine = mine.astype(BF16)
    return exchange(jnp.broadcast_to(mine, (32,) + mine.shape), PLANES)


def relation_kernel(packed, rel, rel_state, rel_out, state_out):
    width, count = rel_state.shape
    block = packed.shape[1]
    tiles = -(-count // block)
    rest = count - block * (tiles - 1)

    def update(grads, rows, lanes):
        state = rel_state[rows, lanes] + grads * grads
        state_out[rows, lanes] = state
        rel_out[rows, lanes] = rel[rows, lanes] - REL_RATE * grads / jnp.sqrt(state)

    def full(p, carry):
        for t in range(tiles - 1):
            grads = packed[pl.ds(pl.multiple_of(width * t + p * GROUP, GROUP), GROUP), :].astype(F32)
            rows = pl.ds(pl.multiple_of(p * GROUP, GROUP), GROUP)
            update(grads, rows, slice(block * t, block * (t + 1)))
        return carry

    lax.fori_loop(0, width // GROUP, full, 0)
    first = width * (tiles - 1)
    folded = packed[first : first + FOLD, :].astype(F32)
    for q in range(4):
        stop = min(FOLD * (q + 1), width)
        grads = folded if q == 0 else pltpu.roll(folded, block - q * block // 4, 1)
        lanes = slice(block * (tiles - 1), count)
        update(grads[: stop - FOLD * q, :rest], slice(FOLD * q, stop), lanes)
    if rel_out.shape[1] > count:
        rel_out[:, count:] = jnp.zeros((width, rel_out.shape[1] - count), F32)


def relation_update(pieces, rel, rel_state, lanes):
    width = rel.shape[0]
    return pl.pallas_call(
        relation_kernel,
        out_shape=(
            jax.ShapeDtypeStruct((width, lanes), F32),
            jax.ShapeDtypeStruct(rel_state.shape, F32),
        ),
        compiler_params=pltpu.CompilerParams(vmem_limit_bytes=16 * MIB),
        name="relation_update",
    )(pieces.reshape(-1, pieces.shape[2]), rel, rel_state)


def shards(
    entities,
    entity_state,
    relations,
    relation_state,
    live_blocks,
    dst_blocks,
    relation_ids,
    source_rows,
    target_rows,
    negative_blocks,
):
    block, width = entities.shape
    dom = lax.axis_index("dom")
    here = (dom % 2).astype(jnp.int32)[None]

    def lists_of(r):
        ids = relation_ids[r]
        numbers = [dst_blocks[r], ids // DIGIT, ids % DIGIT, negative_blocks[r].reshape(-1), live_blocks[r]]
        numbers = jnp.concatenate(numbers)
        numbers = jnp.pad(numbers, (0, block - numbers.shape[0]))[None]
        rows = jnp.concatenate([source_rows[r], target_rows[r], numbers])
        return jnp.pad(rows, ((0, LISTS - rows.shape[0]), (0, 0))).astype(BF16)

    weights = entities.T
    own = send(weights.astype(BF16), TURN)
    own, weights, source_rows, target_rows, dst_blocks = together(
        own, weights, source_rows, target_rows, dst_blocks
    )
    lists = send(jnp.concatenate([lists_of(0), lists_of(1)]), TURN)
    kept = send(jnp.concatenate([weights, jnp.broadcast_to(entity_state[None], (8, block))]), TURN)

    count = relations.shape[0]
    lanes = -(-count // block) * block
    rel = jnp.pad(relations.T, ((0, 0), (0, lanes - count)))
    rel_state = relation_state.T

    half, lists, kept = together(gather_sheet(own), lists, kept)
    other = send(half, OTHER)
    now = lists[:LISTS].astype(jnp.int32)
    mine, theirs, lhs, rel_part = run_blocks(now, here, own, rel, half, other)
    rel_pieces = exchange(rel_part.reshape(32, PIECE, block), PLANES)
    summed, rel_pieces = together(mine + send(theirs, OTHER), rel_pieces)
    pieces, rel_mine = together(exchange(summed, SHEETS), z_steps(rel_pieces))
    kept, own = middle(pieces, lhs, kept)
    source = send(jnp.concatenate([own, lists[LISTS:]]), NEXT)
    kept = send(kept, TURN)
    half, source, rel_mine = together(gather_sheet(own), source, z_step(rel_mine, 8, BF16))
    other = send(half, OTHER)
    rel, rel_state = relation_update(spread_relations(rel_mine), rel, rel_state, lanes)
    other, kept = together(other, kept)

    now = source[width:].astype(jnp.int32)
    mine, theirs, lhs, rel_part = run_blocks(now, here, source[:width], rel, half, other)
    rel_pieces = exchange(rel_part.reshape(32, PIECE, block), PLANES)
    summed, lhs = together(mine + send(theirs, OTHER), lhs.astype(BF16))
    summed, rel_pieces = together(summed, rel_pieces)
    rel_mine = jnp.sum(rel_pieces, 0, dtype=F32)
    rel_mine, lhs = together(z_step(z_step(rel_mine, 1, F32), 2, F32), send(lhs, PREVIOUS))
    rel_mine = z_step(z_step(rel_mine, 4, BF16), 8, BF16)
    pieces, rel_mine = together(exchange(summed, SHEETS), rel_mine)
    grads = send(fold(pieces, lhs), TURN)
    rel_sum = spread_relations(rel_mine)
    weights, state = last(grads, kept)
    rel, rel_state = relation_update(rel_sum, rel, rel_state, count)
    return (weights.T, state[0], rel.T, rel_state.T)


def solution(mesh):
    placed = (
        P(AXES, None),
        P(AXES),
        P(),
        P(),
        P(None, AXES),
        P(None, AXES),
        P(None, AXES),
        P(None, AXES, None),
        P(None, AXES, None),
        P(None, AXES, None),
    )
    return jax.shard_map(
        shards,
        mesh=mesh,
        in_specs=placed,
        out_specs=(P(AXES, None), P(AXES), P(), P()),
        check_vma=False,
    )
```

```python
import jax
import jax.numpy as jnp
from jax import lax
from jax.experimental import pallas as pl
from jax.experimental.pallas import tpu as pltpu
from jax.sharding import PartitionSpec as P

AXES = ("dom", "edge")
N_DOM, N_EDGE = 16, 32
ENT_RATE = 0.25
REL_RATE = 0.25
F32, BF16 = jnp.float32, jnp.bfloat16
GROUP = 16
PIECE = 80
FOLD = 112
DIGIT = 32
LISTS = 32
MIB = 1024 * 1024


def coords(v):
    dom, edge = v // N_EDGE, v % N_EDGE
    return edge % 4, (dom // 2) % 4, dom // 8, edge // 4, dom % 2


def place(x, y, z_hi, z_lo, core):
    return ((z_hi * 4 + y) * 2 + core) * N_EDGE + z_lo * 4 + x


def turn(v):
    x, y, z_hi, z_lo, core = coords(v)
    return place(x, z_lo % 4, z_hi, y + 4 * core, z_lo // 4)


def ahead(v):
    dom, edge = v // N_EDGE, v % N_EDGE
    return turn((dom + 1) % N_DOM * N_EDGE + edge)


ALL = range(N_DOM * N_EDGE)
TURN = [(v, turn(v)) for v in ALL]
NEXT = [(turn(v), ahead(v)) for v in ALL]
PREVIOUS = [(target, source) for source, target in NEXT]


OTHER = []
for v in ALL:
    x, y, z_hi, z_lo, core = coords(v)
    OTHER.append((v, place(x, y, z_hi, z_lo, 1 - core)))

PLANES = [[place(c % 4, c // 4 % 4, z // 8, z % 8, c // 16) for c in range(32)] for z in range(16)]
SHEETS = [plane[16 * core : 16 * core + 16] for plane in PLANES for core in range(2)]


def z_pairs(step):
    pairs = []
    for v in ALL:
        x, y, z_hi, z_lo, core = coords(v)
        z = (z_hi * 8 + z_lo) ^ step
        pairs.append((v, place(x, y, z // 8, z % 8, core)))
    return pairs


def send(value, pairs):
    return lax.ppermute(value, AXES, pairs)


def exchange(value, groups):
    return lax.all_to_all(value, AXES, 0, 0, axis_index_groups=groups, tiled=True)


def gather_sheet(own):
    return exchange(jnp.broadcast_to(own, (16,) + own.shape), SHEETS)


def together(*values):
    return lax.optimization_barrier(values)


def nt(a, b):
    return lax.dot_general(a, b, (((1,), (1,)), ((), ())), preferred_element_type=F32)


def nn(a, b):
    return jnp.dot(a, b, preferred_element_type=F32)


def blocks_kernel(
    scal, here, lists, own, rel, half, other, mine_out, theirs_out, lhs_out, rel_out, table, acc, rel_acc, sems
):
    slots = 10
    width, block = own.shape
    mid = width // 2
    copies = [
        pltpu.make_async_copy(src, table.at[pl.ds(16 * i, 16)], sems.at[i])
        for i, src in enumerate((half, other))
    ]
    for copy in copies:
        copy.start()

    def clear(k, carry):
        acc[k] = jnp.zeros((width, block), F32)
        return carry

    lax.fori_loop(0, 32, clear, 0)
    rel_acc[...] = jnp.zeros(rel_acc.shape, F32)
    lhs_out[...] = jnp.zeros(lhs_out.shape, F32)
    for copy in copies:
        copy.wait()

    def near(b):
        return ((b >> 4) ^ here[0]) * 16 + (b & 15)

    both = 2 * block
    rows = lax.broadcasted_iota(jnp.int32, (both, both), 0)
    lanes = lax.broadcasted_iota(jnp.int32, (both, both), 1)
    count = scal[7 * slots]

    def hot(match):
        return jnp.where(match, 1.0, 0.0).astype(BF16)

    def step(i, carry):
        pair = (2 * i, 2 * i + 1)
        live = (1.0, jnp.where(pair[1] < count, 1.0, 0.0))
        sources = jnp.concatenate([lists[pl.ds(j, 1), :] for j in pair], 1)
        targets = jnp.concatenate([lists[pl.ds(slots + j, 1), :] + block * s for s, j in enumerate(pair)], 1)
        src_hot = hot(rows[:block] == sources)
        tgt_hot = hot(rows == targets)
        dsts = [near(scal[j]) for j in pair]
        rel_ids = [scal[slots + j] * DIGIT + scal[2 * slots + j] for j in pair]
        rel_lanes = [rel_id & (block - 1) for rel_id in rel_ids]
        rel_tiles = [pl.ds(pl.multiple_of((rel_id >> 7) * block, block), block) for rel_id in rel_ids]
        rel_hot = hot(lanes == jnp.where(rows < block, rel_lanes[0], rel_lanes[1] + block))
        heads = nn(own[...], src_hot)
        tails = nn(jnp.concatenate([table[dst] for dst in dsts], 1), tgt_hot)
        columns = [
            pltpu.roll(rel[:, tile], (block - lane) & (block - 1), 1)[:, :1]
            for tile, lane in zip(rel_tiles, rel_lanes)
        ]
        op = jnp.concatenate([jnp.broadcast_to(column, (width, block)) for column in columns], 1)
        h_re, h_im = heads[:mid], heads[mid:]
        r_re, r_im = op[:mid], op[mid:]
        query = jnp.concatenate([h_re * r_re - h_im * r_im, h_re * r_im + h_im * r_re], 0).astype(BF16)
        query_f = query.astype(F32)
        query_t = query_f.T.astype(BF16)
        positive = jnp.sum(query_f * tails, 0, keepdims=True)
        live_lanes = jnp.where(lanes[:1] < block, live[0], live[1])
        pos_weight = -jax.nn.sigmoid(-positive) * live_lanes
        neg_grads = []
        for s, j in enumerate(pair):
            negs = [near(scal[3 * slots + 4 * j + n]) for n in range(4)]
            neg_rows = jnp.concatenate([table[n] for n in negs], 1)
            scores = nn(query_t[block * s : block * (s + 1)], neg_rows)
            neg_weight = (jax.nn.sigmoid(scores) * (live[s] / scores.shape[1])).astype(BF16)
            neg_grads.append(nt(neg_rows, neg_weight))
            neg_add = nn(query[:, block * s : block * (s + 1)], neg_weight)
            for t, n in enumerate(negs):
                acc[n] += neg_add[:, block * t : block * (t + 1)]
        grad_query = pos_weight * tails + jnp.concatenate(neg_grads, 1)
        tgt_add = nt((pos_weight * query_f).astype(BF16), tgt_hot)
        g_re, g_im = grad_query[:mid], grad_query[mid:]
        head_grad = jnp.concatenate([g_re * r_re + g_im * r_im, g_im * r_re - g_re * r_im], 0)
        lhs_out[...] += nt(head_grad.astype(BF16), src_hot)
        op_grad = jnp.concatenate([g_re * h_re + g_im * h_im, g_im * h_re - g_re * h_im], 0)
        rel_add = nn(op_grad.astype(BF16), rel_hot)
        for s in range(2):
            acc[dsts[s]] += tgt_add[:, block * s : block * (s + 1)]
            rel_acc[:, rel_tiles[s]] += rel_add[:, block * s : block * (s + 1)]
        return carry

    lax.fori_loop(0, (count + 1) >> 1, step, 0)

    def pack(k, carry):
        mine_out[k] = acc[k].astype(BF16)
        theirs_out[k] = acc[16 + k].astype(BF16)
        return carry

    lax.fori_loop(0, 16, pack, 0)
    tiles = rel_acc.shape[1] // block
    for t in range(tiles - 1):
        rel_out[width * t : width * (t + 1)] = rel_acc[:, block * t : block * (t + 1)].astype(BF16)
    tail = rel_acc[:, block * (tiles - 1) :]
    folded = tail[:FOLD]
    for q in range(1, 4):
        part = tail[FOLD * q : FOLD * (q + 1)]
        if part.shape[0] < FOLD:
            part = jnp.concatenate([part, jnp.zeros((FOLD - part.shape[0], block), F32)], 0)
        folded = folded + pltpu.roll(part, q * block // 4, 1)
    first = width * (tiles - 1)
    rel_out[first : first + FOLD] = folded.astype(BF16)
    rel_out[first + FOLD :] = jnp.zeros((rel_out.shape[0] - first - FOLD, block), BF16)


def run_blocks(lists, here, own, rel, half, other):
    width, block = own.shape
    rel_lanes = rel.shape[1]
    vmem = pl.BlockSpec(memory_space=pltpu.VMEM)
    smem = pl.BlockSpec(memory_space=pltpu.SMEM)
    hbm = pl.BlockSpec(memory_space=pl.ANY)
    return pl.pallas_call(
        blocks_kernel,
        out_shape=(
            jax.ShapeDtypeStruct((16, width, block), BF16),
            jax.ShapeDtypeStruct((16, width, block), BF16),
            jax.ShapeDtypeStruct((width, block), F32),
            jax.ShapeDtypeStruct((32 * PIECE, block), BF16),
        ),
        in_specs=[smem, smem, vmem, vmem, vmem, hbm, hbm],
        out_specs=(vmem, vmem, vmem, vmem),
        scratch_shapes=[
            pltpu.VMEM((32, width, block), BF16),
            pltpu.VMEM((32, width, block), F32),
            pltpu.VMEM((width, rel_lanes), F32),
            pltpu.SemaphoreType.DMA((2,)),
        ],
        compiler_params=pltpu.CompilerParams(vmem_limit_bytes=40 * MIB),
        cost_estimate=pl.CostEstimate(flops=2 * 10**9, bytes_accessed=10**7, transcendentals=10**6),
        name="edge_blocks",
    )(lists[20], here, lists, own, rel, half, other)


def adagrad(grads, kept):
    width = grads.shape[0]
    state = kept[width : width + 1] + jnp.sum(grads * grads, 0, keepdims=True) * (1.0 / width)
    weights = kept[:width] - grads * (ENT_RATE / jnp.sqrt(state))
    return weights, state


def add_pieces(pieces):
    def add(k, total):
        return total + pieces[k].astype(F32)

    return lax.fori_loop(1, pieces.shape[0], add, pieces[0].astype(F32))


def middle_kernel(pieces, lhs, kept, kept_out, table_out):
    width = lhs.shape[0]
    weights, state = adagrad(lhs[...] + add_pieces(pieces), kept[...])
    kept_out[:width] = weights
    kept_out[width:] = jnp.broadcast_to(state, (kept.shape[0] - width, state.shape[1]))
    table_out[...] = weights.astype(BF16)


def middle(pieces, lhs, kept):
    return pl.pallas_call(
        middle_kernel,
        out_shape=(jax.ShapeDtypeStruct(kept.shape, F32), jax.ShapeDtypeStruct(lhs.shape, BF16)),
        compiler_params=pltpu.CompilerParams(vmem_limit_bytes=16 * MIB),
        name="middle_update",
    )(pieces, lhs, kept)


def fold_kernel(pieces, more, out):
    out[...] = (add_pieces(pieces) + more[...].astype(F32)).astype(out.dtype)


def fold(pieces, more):
    return pl.pallas_call(
        fold_kernel,
        out_shape=jax.ShapeDtypeStruct(more.shape, more.dtype),
        compiler_params=pltpu.CompilerParams(vmem_limit_bytes=16 * MIB),
        name="fold_pieces",
    )(pieces, more)


def last_kernel(grads, kept, weights_out, state_out):
    weights, state = adagrad(grads[...].astype(F32), kept[...])
    weights_out[...] = weights
    state_out[...] = state


def last(grads, kept):
    width, block = grads.shape
    return pl.pallas_call(
        last_kernel,
        out_shape=(
            jax.ShapeDtypeStruct((width, block), F32),
            jax.ShapeDtypeStruct((1, block), F32),
        ),
        name="last_update",
    )(grads, kept)


def z_step(total, step, kind):
    mine = total.astype(kind)
    return mine.astype(F32) + send(mine, z_pairs(step)).astype(F32)


def z_steps(total):
    total = jnp.sum(total, 0, dtype=F32)
    for step, kind in ((1, F32), (2, F32), (4, BF16)):
        total = z_step(total, step, kind)
    return total


def spread_relations(mine):
    mine = mine.astype(BF16)
    return exchange(jnp.broadcast_to(mine, (32,) + mine.shape), PLANES)


def relation_kernel(packed, rel, rel_state, rel_out, state_out):
    width, count = rel_state.shape
    block = packed.shape[1]
    tiles = -(-count // block)
    rest = count - block * (tiles - 1)

    def update(grads, rows, lanes):
        state = rel_state[rows, lanes] + grads * grads
        state_out[rows, lanes] = state
        rel_out[rows, lanes] = rel[rows, lanes] - REL_RATE * grads / jnp.sqrt(state)

    def full(p, carry):
        for t in range(tiles - 1):
            grads = packed[pl.ds(pl.multiple_of(width * t + p * GROUP, GROUP), GROUP), :].astype(F32)
            rows = pl.ds(pl.multiple_of(p * GROUP, GROUP), GROUP)
            update(grads, rows, slice(block * t, block * (t + 1)))
        return carry

    lax.fori_loop(0, width // GROUP, full, 0)
    first = width * (tiles - 1)
    folded = packed[first : first + FOLD, :].astype(F32)
    for q in range(4):
        stop = min(FOLD * (q + 1), width)
        grads = folded if q == 0 else pltpu.roll(folded, block - q * block // 4, 1)
        lanes = slice(block * (tiles - 1), count)
        update(grads[: stop - FOLD * q, :rest], slice(FOLD * q, stop), lanes)
    if rel_out.shape[1] > count:
        rel_out[:, count:] = jnp.zeros((width, rel_out.shape[1] - count), F32)


def relation_update(pieces, rel, rel_state, lanes):
    width = rel.shape[0]
    return pl.pallas_call(
        relation_kernel,
        out_shape=(
            jax.ShapeDtypeStruct((width, lanes), F32),
            jax.ShapeDtypeStruct(rel_state.shape, F32),
        ),
        compiler_params=pltpu.CompilerParams(vmem_limit_bytes=16 * MIB),
        name="relation_update",
    )(pieces.reshape(-1, pieces.shape[2]), rel, rel_state)


def shards(
    entities,
    entity_state,
    relations,
    relation_state,
    live_blocks,
    dst_blocks,
    relation_ids,
    source_rows,
    target_rows,
    negative_blocks,
):
    block, width = entities.shape
    dom = lax.axis_index("dom")
    here = (dom % 2).astype(jnp.int32)[None]

    def lists_of(r):
        ids = relation_ids[r]
        numbers = [dst_blocks[r], ids // DIGIT, ids % DIGIT, negative_blocks[r].reshape(-1), live_blocks[r]]
        numbers = jnp.concatenate(numbers)
        numbers = jnp.pad(numbers, (0, block - numbers.shape[0]))[None]
        rows = jnp.concatenate([source_rows[r], target_rows[r], numbers])
        return jnp.pad(rows, ((0, LISTS - rows.shape[0]), (0, 0))).astype(BF16)

    weights = entities.T
    own = send(weights.astype(BF16), TURN)
    own, weights, source_rows, target_rows, dst_blocks = together(
        own, weights, source_rows, target_rows, dst_blocks
    )
    lists = send(jnp.concatenate([lists_of(0), lists_of(1)]), TURN)
    kept = send(jnp.concatenate([weights, jnp.broadcast_to(entity_state[None], (8, block))]), TURN)

    count = relations.shape[0]
    lanes = -(-count // block) * block
    rel = jnp.pad(relations.T, ((0, 0), (0, lanes - count)))
    rel_state = relation_state.T

    half, lists, kept = together(gather_sheet(own), lists, kept)
    other = send(half, OTHER)
    now = lists[:LISTS].astype(jnp.int32)
    mine, theirs, lhs, rel_part = run_blocks(now, here, own, rel, half, other)
    rel_pieces = exchange(rel_part.reshape(32, PIECE, block), PLANES)
    summed, rel_pieces = together(mine + send(theirs, OTHER), rel_pieces)
    pieces, rel_mine = together(exchange(summed, SHEETS), z_steps(rel_pieces))
    kept, own = middle(pieces, lhs, kept)
    source = send(jnp.concatenate([own, lists[LISTS:]]), NEXT)
    kept = send(kept, TURN)
    half, source, rel_mine = together(gather_sheet(own), source, z_step(rel_mine, 8, BF16))
    other = send(half, OTHER)
    rel, rel_state = relation_update(spread_relations(rel_mine), rel, rel_state, lanes)
    other, kept = together(other, kept)

    now = source[width:].astype(jnp.int32)
    mine, theirs, lhs, rel_part = run_blocks(now, here, source[:width], rel, half, other)
    rel_pieces = exchange(rel_part.reshape(32, PIECE, block), PLANES)
    summed, lhs = together(mine + send(theirs, OTHER), lhs.astype(BF16))
    summed, rel_pieces = together(summed, rel_pieces)
    rel_mine = jnp.sum(rel_pieces, 0, dtype=F32)
    rel_mine, lhs = together(z_step(z_step(rel_mine, 1, F32), 2, F32), send(lhs, PREVIOUS))
    rel_mine = z_step(z_step(rel_mine, 4, BF16), 8, BF16)
    pieces, rel_mine = together(exchange(summed, SHEETS), rel_mine)
    grads = send(fold(pieces, lhs), TURN)
    rel, rel_state = relation_update(spread_relations(rel_mine), rel, rel_state, count)
    kept, rel, rel_state = together(kept, rel, rel_state)
    weights, state = last(grads, kept)
    return (weights.T, state[0], rel.T, rel_state.T)


def solution(mesh):
    placed = (
        P(AXES, None),
        P(AXES),
        P(),
        P(),
        P(None, AXES),
        P(None, AXES),
        P(None, AXES),
        P(None, AXES, None),
        P(None, AXES, None),
        P(None, AXES, None),
    )
    return jax.shard_map(
        shards,
        mesh=mesh,
        in_specs=placed,
        out_specs=(P(AXES, None), P(AXES), P(), P()),
        check_vma=False,
    )
```

```python
import jax
import jax.numpy as jnp
from jax import lax
from jax.experimental import pallas as pl
from jax.experimental.pallas import tpu as pltpu
from jax.sharding import PartitionSpec as P

AXES = ("dom", "edge")
N_DOM, N_EDGE = 16, 32
ENT_RATE = 0.25
REL_RATE = 0.25
F32, BF16 = jnp.float32, jnp.bfloat16
GROUP = 16
PIECE = 80
FOLD = 112
DIGIT = 32
LISTS = 32
MIB = 1024 * 1024


def coords(v):
    dom, edge = v // N_EDGE, v % N_EDGE
    return edge % 4, (dom // 2) % 4, dom // 8, edge // 4, dom % 2


def place(x, y, z_hi, z_lo, core):
    return ((z_hi * 4 + y) * 2 + core) * N_EDGE + z_lo * 4 + x


def turn(v):
    x, y, z_hi, z_lo, core = coords(v)
    return place(x, z_lo % 4, z_hi, y + 4 * core, z_lo // 4)


def ahead(v):
    dom, edge = v // N_EDGE, v % N_EDGE
    return turn((dom + 1) % N_DOM * N_EDGE + edge)


ALL = range(N_DOM * N_EDGE)
TURN = [(v, turn(v)) for v in ALL]
NEXT = [(turn(v), ahead(v)) for v in ALL]
PREVIOUS = [(target, source) for source, target in NEXT]


OTHER = []
for v in ALL:
    x, y, z_hi, z_lo, core = coords(v)
    OTHER.append((v, place(x, y, z_hi, z_lo, 1 - core)))

PLANES = [[place(c % 4, c // 4 % 4, z // 8, z % 8, c // 16) for c in range(32)] for z in range(16)]
SHEETS = [plane[16 * core : 16 * core + 16] for plane in PLANES for core in range(2)]


def z_pairs(step):
    pairs = []
    for v in ALL:
        x, y, z_hi, z_lo, core = coords(v)
        z = (z_hi * 8 + z_lo) ^ step
        pairs.append((v, place(x, y, z // 8, z % 8, core)))
    return pairs


def send(value, pairs):
    return lax.ppermute(value, AXES, pairs)


def exchange(value, groups):
    return lax.all_to_all(value, AXES, 0, 0, axis_index_groups=groups, tiled=True)


def gather_sheet(own):
    return exchange(jnp.broadcast_to(own, (16,) + own.shape), SHEETS)


def together(*values):
    return lax.optimization_barrier(values)


def nt(a, b):
    return lax.dot_general(a, b, (((1,), (1,)), ((), ())), preferred_element_type=F32)


def nn(a, b):
    return jnp.dot(a, b, preferred_element_type=F32)


def blocks_kernel(
    scal, here, lists, own, rel, half, other, mine_out, theirs_out, lhs_out, rel_out, table, acc, rel_acc, sems, update=None
):
    slots = 10
    width, block = own.shape
    mid = width // 2
    copies = [
        pltpu.make_async_copy(src, table.at[pl.ds(16 * i, 16)], sems.at[i])
        for i, src in enumerate((half, other))
    ]
    for copy in copies:
        copy.start()
    if update is not None:
        relation_kernel(*update)

    def clear(k, carry):
        acc[k] = jnp.zeros((width, block), F32)
        return carry

    lax.fori_loop(0, 32, clear, 0)
    rel_acc[...] = jnp.zeros(rel_acc.shape, F32)
    lhs_out[...] = jnp.zeros(lhs_out.shape, F32)
    for copy in copies:
        copy.wait()

    def near(b):
        return ((b >> 4) ^ here[0]) * 16 + (b & 15)

    both = 2 * block
    rows = lax.broadcasted_iota(jnp.int32, (both, both), 0)
    lanes = lax.broadcasted_iota(jnp.int32, (both, both), 1)
    count = scal[7 * slots]

    def hot(match):
        return jnp.where(match, 1.0, 0.0).astype(BF16)

    def step(i, carry):
        pair = (2 * i, 2 * i + 1)
        live = (1.0, jnp.where(pair[1] < count, 1.0, 0.0))
        sources = jnp.concatenate([lists[pl.ds(j, 1), :] for j in pair], 1)
        targets = jnp.concatenate([lists[pl.ds(slots + j, 1), :] + block * s for s, j in enumerate(pair)], 1)
        src_hot = hot(rows[:block] == sources)
        tgt_hot = hot(rows == targets)
        dsts = [near(scal[j]) for j in pair]
        rel_ids = [scal[slots + j] * DIGIT + scal[2 * slots + j] for j in pair]
        rel_lanes = [rel_id & (block - 1) for rel_id in rel_ids]
        rel_tiles = [pl.ds(pl.multiple_of((rel_id >> 7) * block, block), block) for rel_id in rel_ids]
        rel_hot = hot(lanes == jnp.where(rows < block, rel_lanes[0], rel_lanes[1] + block))
        heads = nn(own[...], src_hot)
        tails = nn(jnp.concatenate([table[dst] for dst in dsts], 1), tgt_hot)
        columns = [
            pltpu.roll(rel[:, tile], (block - lane) & (block - 1), 1)[:, :1]
            for tile, lane in zip(rel_tiles, rel_lanes)
        ]
        op = jnp.concatenate([jnp.broadcast_to(column, (width, block)) for column in columns], 1)
        h_re, h_im = heads[:mid], heads[mid:]
        r_re, r_im = op[:mid], op[mid:]
        query = jnp.concatenate([h_re * r_re - h_im * r_im, h_re * r_im + h_im * r_re], 0).astype(BF16)
        query_f = query.astype(F32)
        query_t = query_f.T.astype(BF16)
        positive = jnp.sum(query_f * tails, 0, keepdims=True)
        live_lanes = jnp.where(lanes[:1] < block, live[0], live[1])
        pos_weight = -jax.nn.sigmoid(-positive) * live_lanes
        neg_grads = []
        for s, j in enumerate(pair):
            negs = [near(scal[3 * slots + 4 * j + n]) for n in range(4)]
            neg_rows = jnp.concatenate([table[n] for n in negs], 1)
            scores = nn(query_t[block * s : block * (s + 1)], neg_rows)
            neg_weight = (jax.nn.sigmoid(scores) * (live[s] / scores.shape[1])).astype(BF16)
            neg_grads.append(nt(neg_rows, neg_weight))
            neg_add = nn(query[:, block * s : block * (s + 1)], neg_weight)
            for t, n in enumerate(negs):
                acc[n] += neg_add[:, block * t : block * (t + 1)]
        grad_query = pos_weight * tails + jnp.concatenate(neg_grads, 1)
        tgt_add = nt((pos_weight * query_f).astype(BF16), tgt_hot)
        g_re, g_im = grad_query[:mid], grad_query[mid:]
        head_grad = jnp.concatenate([g_re * r_re + g_im * r_im, g_im * r_re - g_re * r_im], 0)
        lhs_out[...] += nt(head_grad.astype(BF16), src_hot)
        op_grad = jnp.concatenate([g_re * h_re + g_im * h_im, g_im * h_re - g_re * h_im], 0)
        rel_add = nn(op_grad.astype(BF16), rel_hot)
        for s in range(2):
            acc[dsts[s]] += tgt_add[:, block * s : block * (s + 1)]
            rel_acc[:, rel_tiles[s]] += rel_add[:, block * s : block * (s + 1)]
        return carry

    lax.fori_loop(0, (count + 1) >> 1, step, 0)

    def pack(k, carry):
        mine_out[k] = acc[k].astype(BF16)
        theirs_out[k] = acc[16 + k].astype(BF16)
        return carry

    lax.fori_loop(0, 16, pack, 0)
    tiles = rel_acc.shape[1] // block
    for t in range(tiles - 1):
        rel_out[width * t : width * (t + 1)] = rel_acc[:, block * t : block * (t + 1)].astype(BF16)
    tail = rel_acc[:, block * (tiles - 1) :]
    folded = tail[:FOLD]
    for q in range(1, 4):
        part = tail[FOLD * q : FOLD * (q + 1)]
        if part.shape[0] < FOLD:
            part = jnp.concatenate([part, jnp.zeros((FOLD - part.shape[0], block), F32)], 0)
        folded = folded + pltpu.roll(part, q * block // 4, 1)
    first = width * (tiles - 1)
    rel_out[first : first + FOLD] = folded.astype(BF16)
    rel_out[first + FOLD :] = jnp.zeros((rel_out.shape[0] - first - FOLD, block), BF16)


def updating_kernel(
    scal, here, lists, own, rel, half, other, packed, rel_state,
    mine_out, theirs_out, lhs_out, rel_out, new_rel, new_state,
    table, acc, rel_acc, sems,
):
    blocks_kernel(
        scal, here, lists, own, new_rel, half, other, mine_out, theirs_out, lhs_out, rel_out, table, acc, rel_acc, sems,
        update=(packed, rel, rel_state, new_rel, new_state),
    )


def run_blocks(lists, here, own, rel, half, other, rel_sum=None, rel_state=None):
    width, block = own.shape
    vmem = pl.BlockSpec(memory_space=pltpu.VMEM)
    smem = pl.BlockSpec(memory_space=pltpu.SMEM)
    hbm = pl.BlockSpec(memory_space=pl.ANY)
    kernel, more, out_shape = blocks_kernel, [], [
        jax.ShapeDtypeStruct((16, width, block), BF16),
        jax.ShapeDtypeStruct((16, width, block), BF16),
        jax.ShapeDtypeStruct((width, block), F32),
        jax.ShapeDtypeStruct((32 * PIECE, block), BF16),
    ]
    if rel_sum is not None:
        kernel, more = updating_kernel, [rel_sum.reshape(-1, block), rel_state]
        out_shape = out_shape + [
            jax.ShapeDtypeStruct(rel.shape, F32),
            jax.ShapeDtypeStruct(rel_state.shape, F32),
        ]
    return pl.pallas_call(
        kernel,
        out_shape=out_shape,
        in_specs=[smem, smem, vmem, vmem, vmem, hbm, hbm] + [vmem] * len(more),
        out_specs=[vmem] * len(out_shape),
        scratch_shapes=[
            pltpu.VMEM((32, width, block), BF16),
            pltpu.VMEM((32, width, block), F32),
            pltpu.VMEM((width, rel.shape[1]), F32),
            pltpu.SemaphoreType.DMA((2,)),
        ],
        compiler_params=pltpu.CompilerParams(vmem_limit_bytes=44 * MIB),
        cost_estimate=pl.CostEstimate(flops=2 * 10**9, bytes_accessed=10**7, transcendentals=10**6),
        name="edge_blocks",
    )(lists[20], here, lists, own, rel, half, other, *more)


def adagrad(grads, kept):
    width = grads.shape[0]
    state = kept[width : width + 1] + jnp.sum(grads * grads, 0, keepdims=True) * (1.0 / width)
    weights = kept[:width] - grads * (ENT_RATE / jnp.sqrt(state))
    return weights, state


def add_pieces(pieces):
    def add(k, total):
        return total + pieces[k].astype(F32)

    return lax.fori_loop(1, pieces.shape[0], add, pieces[0].astype(F32))


def middle_kernel(pieces, lhs, kept, kept_out, table_out, copies_out):
    width = lhs.shape[0]
    weights, state = adagrad(lhs[...] + add_pieces(pieces), kept[...])
    kept_out[:width] = weights
    kept_out[width:] = jnp.broadcast_to(state, (kept.shape[0] - width, state.shape[1]))
    table = weights.astype(BF16)
    table_out[...] = table
    for k in range(copies_out.shape[0]):
        copies_out[k] = table


def middle(pieces, lhs, kept):
    return pl.pallas_call(
        middle_kernel,
        out_shape=(
            jax.ShapeDtypeStruct(kept.shape, F32),
            jax.ShapeDtypeStruct(lhs.shape, BF16),
            jax.ShapeDtypeStruct((16,) + lhs.shape, BF16),
        ),
        compiler_params=pltpu.CompilerParams(vmem_limit_bytes=16 * MIB),
        name="middle_update",
    )(pieces, lhs, kept)


def fold_kernel(pieces, more, out):
    out[...] = (add_pieces(pieces) + more[...].astype(F32)).astype(out.dtype)


def fold(pieces, more):
    return pl.pallas_call(
        fold_kernel,
        out_shape=jax.ShapeDtypeStruct(more.shape, more.dtype),
        compiler_params=pltpu.CompilerParams(vmem_limit_bytes=16 * MIB),
        name="fold_pieces",
    )(pieces, more)


def last_kernel(grads, kept, weights_out, state_out):
    weights, state = adagrad(grads[...].astype(F32), kept[...])
    weights_out[...] = weights
    state_out[...] = state


def last(grads, kept):
    width, block = grads.shape
    return pl.pallas_call(
        last_kernel,
        out_shape=(
            jax.ShapeDtypeStruct((width, block), F32),
            jax.ShapeDtypeStruct((1, block), F32),
        ),
        name="last_update",
    )(grads, kept)


def z_step(total, step, kind):
    mine = total.astype(kind)
    return mine.astype(F32) + send(mine, z_pairs(step)).astype(F32)


def z_steps(total):
    total = jnp.sum(total, 0, dtype=F32)
    for step, kind in ((1, F32), (2, F32), (4, BF16)):
        total = z_step(total, step, kind)
    return total


def spread_relations(mine):
    mine = mine.astype(BF16)
    return exchange(jnp.broadcast_to(mine, (32,) + mine.shape), PLANES)


def relation_kernel(packed, rel, rel_state, rel_out, state_out):
    width, count = rel_state.shape
    block = packed.shape[1]
    tiles = -(-count // block)
    rest = count - block * (tiles - 1)

    def update(grads, rows, lanes):
        state = rel_state[rows, lanes] + grads * grads
        state_out[rows, lanes] = state
        rel_out[rows, lanes] = rel[rows, lanes] - REL_RATE * grads / jnp.sqrt(state)

    def full(p, carry):
        for t in range(tiles - 1):
            grads = packed[pl.ds(pl.multiple_of(width * t + p * GROUP, GROUP), GROUP), :].astype(F32)
            rows = pl.ds(pl.multiple_of(p * GROUP, GROUP), GROUP)
            update(grads, rows, slice(block * t, block * (t + 1)))
        return carry

    lax.fori_loop(0, width // GROUP, full, 0)
    first = width * (tiles - 1)
    folded = packed[first : first + FOLD, :].astype(F32)
    for q in range(4):
        stop = min(FOLD * (q + 1), width)
        grads = folded if q == 0 else pltpu.roll(folded, block - q * block // 4, 1)
        lanes = slice(block * (tiles - 1), count)
        update(grads[: stop - FOLD * q, :rest], slice(FOLD * q, stop), lanes)
    if rel_out.shape[1] > count:
        rel_out[:, count:] = jnp.zeros((width, rel_out.shape[1] - count), F32)


def relation_update(pieces, rel, rel_state, lanes):
    width = rel.shape[0]
    return pl.pallas_call(
        relation_kernel,
        out_shape=(
            jax.ShapeDtypeStruct((width, lanes), F32),
            jax.ShapeDtypeStruct(rel_state.shape, F32),
        ),
        compiler_params=pltpu.CompilerParams(vmem_limit_bytes=16 * MIB),
        name="relation_update",
    )(pieces.reshape(-1, pieces.shape[2]), rel, rel_state)


def shards(
    entities,
    entity_state,
    relations,
    relation_state,
    live_blocks,
    dst_blocks,
    relation_ids,
    source_rows,
    target_rows,
    negative_blocks,
):
    block, width = entities.shape
    dom = lax.axis_index("dom")
    here = (dom % 2).astype(jnp.int32)[None]

    def lists_of(r):
        ids = relation_ids[r]
        numbers = [dst_blocks[r], ids // DIGIT, ids % DIGIT, negative_blocks[r].reshape(-1), live_blocks[r]]
        numbers = jnp.concatenate(numbers)
        numbers = jnp.pad(numbers, (0, block - numbers.shape[0]))[None]
        rows = jnp.concatenate([source_rows[r], target_rows[r], numbers])
        return jnp.pad(rows, ((0, LISTS - rows.shape[0]), (0, 0))).astype(BF16)

    weights = entities.T
    own = send(weights.astype(BF16), TURN)
    own, weights, source_rows, target_rows, dst_blocks = together(
        own, weights, source_rows, target_rows, dst_blocks
    )
    lists = send(jnp.concatenate([lists_of(0), lists_of(1)]), TURN)
    kept = send(jnp.concatenate([weights, jnp.broadcast_to(entity_state[None], (8, block))]), TURN)

    count = relations.shape[0]
    lanes = -(-count // block) * block
    rel = jnp.pad(relations.T, ((0, 0), (0, lanes - count)))
    rel_state = relation_state.T

    half, lists, kept = together(gather_sheet(own), lists, kept)
    other = send(half, OTHER)
    now = lists[:LISTS].astype(jnp.int32)
    mine, theirs, lhs, rel_part = run_blocks(now, here, own, rel, half, other)
    rel_pieces = exchange(rel_part.reshape(32, PIECE, block), PLANES)
    summed, rel_pieces = together(mine + send(theirs, OTHER), rel_pieces)
    pieces, rel_mine = together(exchange(summed, SHEETS), z_steps(rel_pieces))
    kept, own, copies = middle(pieces, lhs, kept)
    source = send(jnp.concatenate([own, lists[LISTS:]]), NEXT)
    kept = send(kept, TURN)
    half, source, rel_mine = together(exchange(copies, SHEETS), source, z_step(rel_mine, 8, BF16))
    other = send(half, OTHER)
    rel_sum = spread_relations(rel_mine)
    other, kept = together(other, kept)

    now = source[width:].astype(jnp.int32)
    mine, theirs, lhs, rel_part, rel, rel_state = run_blocks(
        now, here, source[:width], rel, half, other, rel_sum, rel_state
    )
    rel_pieces = exchange(rel_part.reshape(32, PIECE, block), PLANES)
    summed, lhs = together(mine + send(theirs, OTHER), lhs.astype(BF16))
    summed, rel_pieces = together(summed, rel_pieces)
    rel_mine = jnp.sum(rel_pieces, 0, dtype=F32)
    rel_mine, lhs = together(z_step(z_step(rel_mine, 1, F32), 2, F32), send(lhs, PREVIOUS))
    rel_mine = z_step(z_step(rel_mine, 4, BF16), 8, BF16)
    pieces, rel_mine = together(exchange(summed, SHEETS), rel_mine)
    grads = send(fold(pieces, lhs), TURN)
    rel, rel_state = relation_update(spread_relations(rel_mine), rel, rel_state, count)
    kept, rel, rel_state = together(kept, rel, rel_state)
    weights, state = last(grads, kept)
    return (weights.T, state[0], rel.T, rel_state.T)


def solution(mesh):
    placed = (
        P(AXES, None),
        P(AXES),
        P(),
        P(),
        P(None, AXES),
        P(None, AXES),
        P(None, AXES),
        P(None, AXES, None),
        P(None, AXES, None),
        P(None, AXES, None),
    )
    return jax.shard_map(
        shards,
        mesh=mesh,
        in_specs=placed,
        out_specs=(P(AXES, None), P(AXES), P(), P()),
        check_vma=False,
    )
```

```python
import jax
import jax.numpy as jnp
from jax import lax
from jax.experimental import pallas as pl
from jax.experimental.pallas import tpu as pltpu
from jax.sharding import PartitionSpec as P

AXES = ("dom", "edge")
N_DOM, N_EDGE = 16, 32
ENT_RATE = 0.25
REL_RATE = 0.25
F32, BF16 = jnp.float32, jnp.bfloat16
GROUP = 16
PIECE = 80
FOLD = 112
DIGIT = 32
LISTS = 32
MIB = 1024 * 1024


def coords(v):
    dom, edge = v // N_EDGE, v % N_EDGE
    return edge % 4, (dom // 2) % 4, dom // 8, edge // 4, dom % 2


def place(x, y, z_hi, z_lo, core):
    return ((z_hi * 4 + y) * 2 + core) * N_EDGE + z_lo * 4 + x


def turn(v):
    x, y, z_hi, z_lo, core = coords(v)
    return place(x, z_lo % 4, z_hi, y + 4 * core, z_lo // 4)


def ahead(v):
    dom, edge = v // N_EDGE, v % N_EDGE
    return turn((dom + 1) % N_DOM * N_EDGE + edge)


ALL = range(N_DOM * N_EDGE)
TURN = [(v, turn(v)) for v in ALL]
NEXT = [(turn(v), ahead(v)) for v in ALL]
PREVIOUS = [(target, source) for source, target in NEXT]


OTHER = []
for v in ALL:
    x, y, z_hi, z_lo, core = coords(v)
    OTHER.append((v, place(x, y, z_hi, z_lo, 1 - core)))

PLANES = [[place(c % 4, c // 4 % 4, z // 8, z % 8, c // 16) for c in range(32)] for z in range(16)]
SHEETS = [plane[16 * core : 16 * core + 16] for plane in PLANES for core in range(2)]


def z_pairs(step):
    pairs = []
    for v in ALL:
        x, y, z_hi, z_lo, core = coords(v)
        z = (z_hi * 8 + z_lo) ^ step
        pairs.append((v, place(x, y, z // 8, z % 8, core)))
    return pairs


def send(value, pairs):
    return lax.ppermute(value, AXES, pairs)


def exchange(value, groups):
    return lax.all_to_all(value, AXES, 0, 0, axis_index_groups=groups, tiled=True)


def gather_sheet(own):
    return exchange(jnp.broadcast_to(own, (16,) + own.shape), SHEETS)


def together(*values):
    return lax.optimization_barrier(values)


def nt(a, b):
    return lax.dot_general(a, b, (((1,), (1,)), ((), ())), preferred_element_type=F32)


def nn(a, b):
    return jnp.dot(a, b, preferred_element_type=F32)


def blocks_kernel(
    scal, here, lists, own, rel, half, other, mine_out, theirs_out, lhs_out, rel_out, table, acc, rel_acc, sems
):
    slots = 10
    width, block = own.shape
    mid = width // 2
    copies = [
        pltpu.make_async_copy(src, table.at[pl.ds(16 * i, 16)], sems.at[i])
        for i, src in enumerate((half, other))
    ]
    for copy in copies:
        copy.start()

    def clear(k, carry):
        acc[k] = jnp.zeros((width, block), F32)
        return carry

    lax.fori_loop(0, 32, clear, 0)
    rel_acc[...] = jnp.zeros(rel_acc.shape, F32)
    lhs_out[...] = jnp.zeros(lhs_out.shape, F32)
    for copy in copies:
        copy.wait()

    def near(b):
        return ((b >> 4) ^ here[0]) * 16 + (b & 15)

    both = 2 * block
    rows = lax.broadcasted_iota(jnp.int32, (both, both), 0)
    lanes = lax.broadcasted_iota(jnp.int32, (both, both), 1)
    count = scal[7 * slots]

    def hot(match):
        return jnp.where(match, 1.0, 0.0).astype(BF16)

    def step(i, carry):
        pair = (2 * i, 2 * i + 1)
        live = (1.0, jnp.where(pair[1] < count, 1.0, 0.0))
        sources = jnp.concatenate([lists[pl.ds(j, 1), :] for j in pair], 1)
        targets = jnp.concatenate([lists[pl.ds(slots + j, 1), :] + block * s for s, j in enumerate(pair)], 1)
        src_hot = hot(rows[:block] == sources)
        tgt_hot = hot(rows == targets)
        dsts = [near(scal[j]) for j in pair]
        rel_ids = [scal[slots + j] * DIGIT + scal[2 * slots + j] for j in pair]
        rel_lanes = [rel_id & (block - 1) for rel_id in rel_ids]
        rel_tiles = [pl.ds(pl.multiple_of((rel_id >> 7) * block, block), block) for rel_id in rel_ids]
        rel_hot = hot(lanes == jnp.where(rows < block, rel_lanes[0], rel_lanes[1] + block))
        heads = nn(own[...], src_hot)
        tails = nn(jnp.concatenate([table[dst] for dst in dsts], 1), tgt_hot)
        columns = [
            pltpu.roll(rel[:, tile], (block - lane) & (block - 1), 1)[:, :1]
            for tile, lane in zip(rel_tiles, rel_lanes)
        ]
        op = jnp.concatenate([jnp.broadcast_to(column, (width, block)) for column in columns], 1)
        h_re, h_im = heads[:mid], heads[mid:]
        r_re, r_im = op[:mid], op[mid:]
        query = jnp.concatenate([h_re * r_re - h_im * r_im, h_re * r_im + h_im * r_re], 0).astype(BF16)
        query_f = query.astype(F32)
        query_t = query_f.T.astype(BF16)
        positive = jnp.sum(query_f * tails, 0, keepdims=True)
        live_lanes = jnp.where(lanes[:1] < block, live[0], live[1])
        pos_weight = -jax.nn.sigmoid(-positive) * live_lanes
        neg_grads = []
        for s, j in enumerate(pair):
            negs = [near(scal[3 * slots + 4 * j + n]) for n in range(4)]
            neg_rows = jnp.concatenate([table[n] for n in negs], 1)
            scores = nn(query_t[block * s : block * (s + 1)], neg_rows)
            neg_weight = (jax.nn.sigmoid(scores) * (live[s] / scores.shape[1])).astype(BF16)
            neg_grads.append(nt(neg_rows, neg_weight))
            neg_add = nn(query[:, block * s : block * (s + 1)], neg_weight)
            for t, n in enumerate(negs):
                acc[n] += neg_add[:, block * t : block * (t + 1)]
        grad_query = pos_weight * tails + jnp.concatenate(neg_grads, 1)
        tgt_add = nt((pos_weight * query_f).astype(BF16), tgt_hot)
        g_re, g_im = grad_query[:mid], grad_query[mid:]
        head_grad = jnp.concatenate([g_re * r_re + g_im * r_im, g_im * r_re - g_re * r_im], 0)
        lhs_out[...] += nt(head_grad.astype(BF16), src_hot)
        op_grad = jnp.concatenate([g_re * h_re + g_im * h_im, g_im * h_re - g_re * h_im], 0)
        rel_add = nn(op_grad.astype(BF16), rel_hot)
        for s in range(2):
            acc[dsts[s]] += tgt_add[:, block * s : block * (s + 1)]
            rel_acc[:, rel_tiles[s]] += rel_add[:, block * s : block * (s + 1)]
        return carry

    lax.fori_loop(0, (count + 1) >> 1, step, 0)

    def pack(k, carry):
        mine_out[k] = acc[k].astype(BF16)
        theirs_out[k] = acc[16 + k].astype(BF16)
        return carry

    lax.fori_loop(0, 16, pack, 0)
    tiles = rel_acc.shape[1] // block
    for t in range(tiles - 1):
        rel_out[width * t : width * (t + 1)] = rel_acc[:, block * t : block * (t + 1)].astype(BF16)
    tail = rel_acc[:, block * (tiles - 1) :]
    folded = tail[:FOLD]
    for q in range(1, 4):
        part = tail[FOLD * q : FOLD * (q + 1)]
        if part.shape[0] < FOLD:
            part = jnp.concatenate([part, jnp.zeros((FOLD - part.shape[0], block), F32)], 0)
        folded = folded + pltpu.roll(part, q * block // 4, 1)
    first = width * (tiles - 1)
    rel_out[first : first + FOLD] = folded.astype(BF16)
    rel_out[first + FOLD :] = jnp.zeros((rel_out.shape[0] - first - FOLD, block), BF16)


def run_blocks(lists, here, own, rel, half, other):
    width, block = own.shape
    rel_lanes = rel.shape[1]
    vmem = pl.BlockSpec(memory_space=pltpu.VMEM)
    smem = pl.BlockSpec(memory_space=pltpu.SMEM)
    hbm = pl.BlockSpec(memory_space=pl.ANY)
    return pl.pallas_call(
        blocks_kernel,
        out_shape=(
            jax.ShapeDtypeStruct((16, width, block), BF16),
            jax.ShapeDtypeStruct((16, width, block), BF16),
            jax.ShapeDtypeStruct((width, block), F32),
            jax.ShapeDtypeStruct((32 * PIECE, block), BF16),
        ),
        in_specs=[smem, smem, vmem, vmem, vmem, hbm, hbm],
        out_specs=(vmem, vmem, vmem, vmem),
        scratch_shapes=[
            pltpu.VMEM((32, width, block), BF16),
            pltpu.VMEM((32, width, block), F32),
            pltpu.VMEM((width, rel_lanes), F32),
            pltpu.SemaphoreType.DMA((2,)),
        ],
        compiler_params=pltpu.CompilerParams(vmem_limit_bytes=40 * MIB),
        cost_estimate=pl.CostEstimate(flops=2 * 10**9, bytes_accessed=10**7, transcendentals=10**6),
        name="edge_blocks",
    )(lists[20], here, lists, own, rel, half, other)


def adagrad(grads, kept):
    width = grads.shape[0]
    state = kept[width : width + 1] + jnp.sum(grads * grads, 0, keepdims=True) * (1.0 / width)
    weights = kept[:width] - grads * (ENT_RATE / jnp.sqrt(state))
    return weights, state


def add_pieces(pieces):
    def add(k, total):
        return total + pieces[k].astype(F32)

    return lax.fori_loop(1, pieces.shape[0], add, pieces[0].astype(F32))


def middle_kernel(pieces, lhs, kept, kept_out, table_out):
    width = lhs.shape[0]
    weights, state = adagrad(lhs[...] + add_pieces(pieces), kept[...])
    kept_out[:width] = weights
    kept_out[width:] = jnp.broadcast_to(state, (kept.shape[0] - width, state.shape[1]))
    table_out[...] = weights.astype(BF16)


def middle(pieces, lhs, kept):
    return pl.pallas_call(
        middle_kernel,
        out_shape=(jax.ShapeDtypeStruct(kept.shape, F32), jax.ShapeDtypeStruct(lhs.shape, BF16)),
        compiler_params=pltpu.CompilerParams(vmem_limit_bytes=16 * MIB),
        name="middle_update",
    )(pieces, lhs, kept)


def fold_kernel(pieces, more, out):
    out[...] = (add_pieces(pieces) + more[...].astype(F32)).astype(out.dtype)


def fold(pieces, more):
    return pl.pallas_call(
        fold_kernel,
        out_shape=jax.ShapeDtypeStruct(more.shape, more.dtype),
        compiler_params=pltpu.CompilerParams(vmem_limit_bytes=16 * MIB),
        name="fold_pieces",
    )(pieces, more)


def last_kernel(grads, kept, weights_out, state_out):
    weights, state = adagrad(grads[...].astype(F32), kept[...])
    weights_out[...] = weights
    state_out[...] = state


def last(grads, kept):
    width, block = grads.shape
    return pl.pallas_call(
        last_kernel,
        out_shape=(
            jax.ShapeDtypeStruct((width, block), F32),
            jax.ShapeDtypeStruct((1, block), F32),
        ),
        name="last_update",
    )(grads, kept)


def z_step(total, step, kind):
    mine = total.astype(kind)
    return mine.astype(F32) + send(mine, z_pairs(step)).astype(F32)


def z_steps(total):
    total = jnp.sum(total, 0, dtype=F32)
    for step, kind in ((1, F32), (2, F32), (4, BF16)):
        total = z_step(total, step, kind)
    return total


def spread_relations(mine):
    mine = mine.astype(BF16)
    return exchange(jnp.broadcast_to(mine, (32,) + mine.shape), PLANES)


def relation_kernel(packed, rel, rel_state, rel_out, state_out):
    width, count = rel_state.shape
    block = packed.shape[1]
    tiles = -(-count // block)
    rest = count - block * (tiles - 1)

    def update(grads, rows, lanes):
        state = rel_state[rows, lanes] + grads * grads
        state_out[rows, lanes] = state
        rel_out[rows, lanes] = rel[rows, lanes] - REL_RATE * grads / jnp.sqrt(state)

    def full(p, carry):
        for t in range(tiles - 1):
            grads = packed[pl.ds(pl.multiple_of(width * t + p * GROUP, GROUP), GROUP), :].astype(F32)
            rows = pl.ds(pl.multiple_of(p * GROUP, GROUP), GROUP)
            update(grads, rows, slice(block * t, block * (t + 1)))
        return carry

    lax.fori_loop(0, width // GROUP, full, 0)
    first = width * (tiles - 1)
    folded = packed[first : first + FOLD, :].astype(F32)
    for q in range(4):
        stop = min(FOLD * (q + 1), width)
        grads = folded if q == 0 else pltpu.roll(folded, block - q * block // 4, 1)
        lanes = slice(block * (tiles - 1), count)
        update(grads[: stop - FOLD * q, :rest], slice(FOLD * q, stop), lanes)
    if rel_out.shape[1] > count:
        rel_out[:, count:] = jnp.zeros((width, rel_out.shape[1] - count), F32)


def relation_update(pieces, rel, rel_state, lanes):
    width = rel.shape[0]
    return pl.pallas_call(
        relation_kernel,
        out_shape=(
            jax.ShapeDtypeStruct((width, lanes), F32),
            jax.ShapeDtypeStruct(rel_state.shape, F32),
        ),
        compiler_params=pltpu.CompilerParams(vmem_limit_bytes=16 * MIB),
        name="relation_update",
    )(pieces.reshape(-1, pieces.shape[2]), rel, rel_state)


def shards(
    entities,
    entity_state,
    relations,
    relation_state,
    live_blocks,
    dst_blocks,
    relation_ids,
    source_rows,
    target_rows,
    negative_blocks,
):
    block, width = entities.shape
    dom = lax.axis_index("dom")
    here = (dom % 2).astype(jnp.int32)[None]

    def lists_of(r):
        ids = relation_ids[r]
        numbers = [dst_blocks[r], ids // DIGIT, ids % DIGIT, negative_blocks[r].reshape(-1), live_blocks[r]]
        numbers = jnp.concatenate(numbers)
        numbers = jnp.pad(numbers, (0, block - numbers.shape[0]))[None]
        rows = jnp.concatenate([source_rows[r], target_rows[r], numbers])
        return jnp.pad(rows, ((0, LISTS - rows.shape[0]), (0, 0))).astype(BF16)

    weights = entities.T
    own = send(weights.astype(BF16), TURN)
    own, weights, source_rows, target_rows, dst_blocks = together(
        own, weights, source_rows, target_rows, dst_blocks
    )
    lists = send(jnp.concatenate([lists_of(0), lists_of(1)]), TURN)
    kept = send(jnp.concatenate([weights, jnp.broadcast_to(entity_state[None], (8, block))]), TURN)

    count = relations.shape[0]
    lanes = -(-count // block) * block
    rel = jnp.pad(relations.T, ((0, 0), (0, lanes - count)))
    rel_state = relation_state.T

    half, lists, kept = together(gather_sheet(own), lists, kept)
    other = send(half, OTHER)
    now = lists[:LISTS].astype(jnp.int32)
    mine, theirs, lhs, rel_part = run_blocks(now, here, own, rel, half, other)
    rel_pieces = exchange(rel_part.reshape(32, PIECE, block), PLANES)
    summed, rel_pieces = together(mine + send(theirs, OTHER), rel_pieces)
    pieces, rel_mine = together(exchange(summed, SHEETS), z_steps(rel_pieces))
    kept, own = middle(pieces, lhs, kept)
    source = send(jnp.concatenate([own, lists[LISTS:]]), NEXT)
    kept = send(kept, TURN)
    half, source, rel_mine = together(gather_sheet(own), source, z_step(rel_mine, 8, BF16))
    other = send(half, OTHER)
    rel, rel_state = relation_update(spread_relations(rel_mine), rel, rel_state, lanes)
    other, kept = together(other, kept)

    now = source[width:].astype(jnp.int32)
    mine, theirs, lhs, rel_part = run_blocks(now, here, source[:width], rel, half, other)
    rel_pieces = exchange(rel_part.reshape(32, PIECE, block), PLANES)
    summed, lhs = together(mine + send(theirs, OTHER), lhs.astype(BF16))
    summed, rel_pieces = together(summed, rel_pieces)
    rel_mine = jnp.sum(rel_pieces, 0, dtype=F32)
    rel_mine, lhs = together(z_step(rel_mine, 1, F32), lhs)
    rel_mine = z_step(z_step(rel_mine, 2, F32), 4, BF16)
    rel_mine, lhs = together(rel_mine, send(lhs, PREVIOUS))
    rel_mine = z_step(rel_mine, 8, BF16)
    pieces, rel_mine = together(exchange(summed, SHEETS), rel_mine)
    grads = send(fold(pieces, lhs), TURN)
    rel, rel_state = relation_update(spread_relations(rel_mine), rel, rel_state, count)
    kept, rel, rel_state = together(kept, rel, rel_state)
    weights, state = last(grads, kept)
    return (weights.T, state[0], rel.T, rel_state.T)


def solution(mesh):
    placed = (
        P(AXES, None),
        P(AXES),
        P(),
        P(),
        P(None, AXES),
        P(None, AXES),
        P(None, AXES),
        P(None, AXES, None),
        P(None, AXES, None),
        P(None, AXES, None),
    )
    return jax.shard_map(
        shards,
        mesh=mesh,
        in_specs=placed,
        out_specs=(P(AXES, None), P(AXES), P(), P()),
        check_vma=False,
    )
```
